256 devices in a mesh: space: 32 (over x, z_lo, core), mode: 8 (over y, z_hi).
Axes of the slice: x: 4, y: 4, z: 8 (z_hi: 2, z_lo: 4; z = z_hi * 4 + z_lo), core: 2. Of those that a mesh axis runs over, the one named last changes fastest.
Arguments:
- field: float32 [56, 128, 48, 128], P('mode', 'space'), may hold values from -6 to 6
- coeff: float32 [6, 128, 48, 128], P(None, 'space'), may hold values from 0.02 to 0.4
- pairs: int32 [6, 168, 2], replicated, may hold values from 0 to 55
- values: float32 [6, 168], replicated, may hold values from -4 to 4
Outputs:
- first: float32 [56, 128, 48, 128], P('mode', 'space')
- second: float32 [56, 128, 48, 128], P('mode', 'space')
The draws below stay inside these ranges and needn't reach their ends.
All inputs are finite; a program needn't handle non-finite values.
Results may differ from the reference program's by a relative error of at most 0.0001.
Values sent between devices are 32-bit elements; how exact they have to be, the bound alone decides.
A program may use at most 64 MiB of HBM per device.

```python
import math
import jax
import jax.numpy as jnp
from jax import lax

P_SIZE = 56
KL = 6
NNZ = 168
NY = 48
NZ = 128
NX = 128


def touch_ends(values, own_key, low, largest):
    shape = values.shape
    place = [jax.random.randint(jax.random.fold_in(own_key, axis), (), 0, shape[axis]) for axis in range(len(shape))]
    values = values.at[tuple(place)].set(low)
    longest = shape.index(max(shape))
    place[longest] = (place[longest] + 1) % shape[longest]
    return values.at[tuple(place)].set(largest)


def block_levels(key, shape, cuts, smallest, largest):
    loudness, own = 1.0, jax.random.fold_in(key, 6)
    for dim, shards_of in cuts:
        steps = jnp.exp(jax.random.uniform(jax.random.fold_in(own, dim), (shards_of,), jnp.float32, smallest / len(cuts), largest / len(cuts)))
        loudness = loudness * jnp.repeat(steps, shape[dim] // shards_of).reshape([-1 if axis == dim else 1 for axis in range(len(shape))])
    return loudness


def noise(own_key, extent, spread, reach, cuts=(), kind=jnp.bfloat16):
    entries = spread * jax.random.normal(own_key, extent, jnp.float32)
    if cuts:
        entries = entries * block_levels(own_key, extent, cuts, -0.22, 0.18)
    return jnp.clip(entries, -reach, reach).astype(kind)


def setup_inputs(seed: int = 0) -> dict:
    key_of = jax.random.split(jax.random.key(seed), 5)
    field = noise(key_of[0], (P_SIZE, NX, NY, NZ), 1.0, 6.0, ((0, 8), (1, 32)), jnp.float32)
    coeff = jnp.clip(jnp.exp(math.log(0.4) - 2.9957323 * jax.random.uniform(key_of[1], (KL, NX, NY, NZ), jnp.float32) ** block_levels(key_of[1], (KL, NX, NY, NZ), ((1, 32),), -0.2, 0.2)), 0.02, 0.4)
    pairs = touch_ends(jax.random.randint(key_of[2], (KL, NNZ, 2), 0, P_SIZE), jax.random.fold_in(key_of[2], 1), 0, P_SIZE - 1).astype(jnp.int32)
    values = noise(key_of[3], (KL, NNZ), 0.3, 4.0, (), jnp.float32)
    return {"field": field, "coeff": coeff, "pairs": pairs, "values": values}


def diffuse(coeff_pad, field_pad):
    a_full = jnp.pad(coeff_pad, ((0, 0), (0, 0), (1, 1), (1, 1)))
    v_full = jnp.pad(field_pad, ((0, 0), (0, 0), (0, 0), (1, 1), (1, 1)))
    size_x = a_full.shape[1] - 2
    size_y = a_full.shape[2] - 2
    size_z = a_full.shape[3] - 2
    center_a = a_full[:, 1:1 + size_x, 1:1 + size_y, 1:1 + size_z][:, None]
    center_v = v_full[:, :, 1:1 + size_x, 1:1 + size_y, 1:1 + size_z]
    summed = jnp.zeros((max(center_a.shape[0], center_v.shape[0]),) + center_v.shape[1:], jnp.float32)
    for step_x, step_y, step_z in ((1, 0, 0), (-1, 0, 0), (0, 1, 0), (0, -1, 0), (0, 0, 1), (0, 0, -1)):
        near_a = a_full[:, 1 + step_x:1 + step_x + size_x, 1 + step_y:1 + step_y + size_y, 1 + step_z:1 + step_z + size_z][:, None]
        near_v = v_full[:, :, 1 + step_x:1 + step_x + size_x, 1 + step_y:1 + step_y + size_y, 1 + step_z:1 + step_z + size_z]
        summed = summed + 0.5 * (center_a + near_a) * (center_v - near_v)
    return summed


def couplings(pairs, values):
    term_ids = jnp.broadcast_to(jnp.arange(KL, dtype=jnp.int32)[:, None], (KL, NNZ))
    dense = jnp.zeros((KL, P_SIZE, P_SIZE), jnp.float32)
    return dense.at[term_ids, pairs[:, :, 0], pairs[:, :, 1]].add(values)


def galerkin(modes, coeff_pad, dense):
    result = jnp.zeros(modes.shape, jnp.float32)
    for term in range(KL):
        mixed = jnp.einsum("ij,jabc->iabc", dense[term], modes, precision=lax.Precision.HIGHEST)
        mixed_pad = jnp.pad(mixed, ((0, 0), (1, 1), (0, 0), (0, 0)))
        result = result + diffuse(coeff_pad[term:term + 1], mixed_pad[None])[0]
    return result


def reference(field, coeff, pairs, values):
    dense = couplings(pairs, values)
    coeff_pad = jnp.pad(coeff, ((0, 0), (1, 1), (0, 0), (0, 0)))
    first = galerkin(field, coeff_pad, dense)
    second = galerkin(first, coeff_pad, dense)
    return first, second
```

```python
import functools

import jax
import jax.numpy as jnp
from jax import lax
from jax.experimental import pallas as pl
from jax.experimental.pallas import tpu as pltpu
from jax.sharding import PartitionSpec as P

MESH = pl.DeviceIdType.MESH
F32 = jnp.float32
BF16 = jnp.bfloat16

TERMS = 6
OWN = 7
SIDE = 28
MODES = 56
LAYERS = 4
ROWS = 12
CELLS = LAYERS * ROWS
FACES = 6
HIGH_ROWS = ROWS + 2


def kernel(
    field,
    coeff,
    pairs,
    values,
    first_out,
    second_out,
    U,
    F,
    S,
    T,
    HX,
    HY,
    A,
    FC,
    O,
    LF,
    L1,
    L2,
    y_send,
    y_recv,
    z_send,
    z_recv,
    c_send,
    c_recv,
    h_send,
    h_recv,
    o_send,
    o_recv,
    loc,
):
    space = lax.axis_index("space")
    mode = lax.axis_index("mode")
    y = mode // 2
    zhi = mode % 2
    z = zhi * 4 + (space // 2) % 4

    def y_peer(step):
        return (space, lax.rem(y + step, 4) * 2 + zhi)

    def z_peer(step):
        at = lax.rem(z + step + 8, 8)
        return ((space // 8) * 8 + lax.rem(at, 4) * 2 + space % 2, y * 2 + at // 4)

    def s_peer(step):
        return (space + step, mode)

    def send(src, dst, ss, rs, dev):
        return pltpu.make_async_remote_copy(
            src_ref=src, dst_ref=dst, send_sem=ss, recv_sem=rs, device_id=dev, device_id_type=MESH
        )

    has_low = space > 0
    has_high = space < 31
    y_low = y > 0
    y_high = y < 3

    U2 = U.reshape(MODES * CELLS, 128)
    F2 = F.reshape(MODES * CELLS, 128)
    S2 = S.reshape(32 * CELLS, 128)
    A2 = A.reshape(TERMS * 6 * HIGH_ROWS, 128)
    FC2 = FC.reshape(CELLS * 36, 128)

    A2[...] = jnp.zeros(A2.shape, F32)
    HX2 = [[HX.at[n, d].reshape(MODES * ROWS, 128) for d in range(2)] for n in range(2)]
    HY2 = [[HY.at[n, d].reshape(MODES * LAYERS, 128) for d in range(2)] for n in range(2)]
    for n in range(2):
        for d, present in ((0, has_low), (1, has_high)):

            @pl.when(jnp.logical_not(present))
            def _(ref=HX2[n][d]):
                ref[...] = jnp.zeros(ref.shape, F32)

        for d, present in ((0, y_low), (1, y_high)):

            @pl.when(jnp.logical_not(present))
            def _(ref=HY2[n][d]):
                ref[...] = jnp.zeros(ref.shape, F32)

    barrier = pltpu.get_barrier_semaphore()
    for step in (1, 2, 3):
        pl.semaphore_signal(barrier, inc=1, device_id=y_peer(step), device_id_type=MESH)
    for step in (1, -1):
        pl.semaphore_signal(barrier, inc=1, device_id=z_peer(step), device_id_type=MESH)

    @pl.when(has_low)
    def _():
        pl.semaphore_signal(barrier, inc=1, device_id=s_peer(-1), device_id_type=MESH)

    @pl.when(has_high)
    def _():
        pl.semaphore_signal(barrier, inc=1, device_id=s_peer(1), device_id_type=MESH)

    pl.semaphore_wait(barrier, 5 + has_low.astype(jnp.int32) + has_high.astype(jnp.int32))

    def y_copy(step, l):
        to = lax.rem(y + step, 4)
        return send(
            field.at[:, l, pl.ds(to * ROWS, ROWS)],
            U.at[pl.ds(zhi * SIDE + y * OWN, OWN), l],
            y_send.at[step, l],
            y_recv.at[step, l],
            y_peer(step),
        )

    def y_arrival(step, l):
        src = lax.rem(y + 4 - step, 4)
        return send(
            field.at[:, l, pl.ds(0, ROWS)],
            U.at[pl.ds(zhi * SIDE + src * OWN, OWN), l],
            y_send.at[step, l],
            y_recv.at[step, l],
            y_peer(step),
        )

    def direction(l, j):
        return 1 - 2 * lax.rem(l + j, 2)

    def block_of(side, j):
        return pl.ds(side * SIDE + lax.rem(y + j, 4) * OWN, OWN)

    def z_copy(hop, l, j, own=False):
        d = direction(l, j)
        c = l * 4 + j
        if hop == 0:
            src = field.at[:, l, pl.ds(y * ROWS, ROWS)] if own else U.at[block_of(zhi, j), l]
        else:
            src = T.at[hop - 1, c]
        if hop < 3:
            dst = T.at[hop, c]
        else:
            side = lax.rem(z - 3 * d + 8, 8) // 4
            dst = U.at[block_of(side, j), l]
        return send(src, dst, z_send.at[hop, c], z_recv.at[hop, c], z_peer(d))

    def z_arrival(hop, l, j):
        d = direction(l, j)
        c = l * 4 + j
        dst = T.at[hop, c] if hop < 3 else U.at[block_of(1 - zhi, j), l]
        return send(T.at[0, c], dst, z_send.at[hop, c], z_recv.at[hop, c], z_peer(-d))

    def loop(n, body):
        def step(i, carry):
            body(i)
            return carry

        lax.fori_loop(0, n, step, 0)

    for l in range(LAYERS):
        z_copy(0, l, 0, own=True).start()
    for l in range(LAYERS):
        for step in (1, 3, 2):
            y_copy(step, l).start()

    own_a = pltpu.make_async_copy(
        coeff.at[:, :, pl.ds(y * ROWS, ROWS)], A.at[:, pl.ds(1, LAYERS), pl.ds(1, ROWS)], loc.at[0]
    )
    own_a.start()
    low_a = pltpu.make_async_copy(
        coeff.at[:, :, pl.ds(jnp.maximum(y * ROWS - 1, 0), 1)],
        A.at[:, pl.ds(1, LAYERS), pl.ds(0, 1)],
        loc.at[1],
    )
    high_a = pltpu.make_async_copy(
        coeff.at[:, :, pl.ds(jnp.minimum(y * ROWS + ROWS, 47), 1)],
        A.at[:, pl.ds(1, LAYERS), pl.ds(ROWS + 1, 1)],
        loc.at[2],
    )
    own_u = pltpu.make_async_copy(
        field.at[:, :, pl.ds(y * ROWS, ROWS)], U.at[pl.ds(zhi * SIDE + y * OWN, OWN)], loc.at[3]
    )
    own_u.start()

    def a_copy(up):
        l, slot, s = (LAYERS - 1, 0, 1) if up else (0, LAYERS + 1, -1)
        return send(
            coeff.at[:, l, pl.ds(y * ROWS, ROWS)],
            A.at[:, slot, pl.ds(1, ROWS)],
            c_send.at[int(up)],
            c_recv.at[int(up)],
            s_peer(s),
        )

    pl.when(y_low)(low_a.start)
    pl.when(y_high)(high_a.start)
    pl.when(has_high)(a_copy(True).start)
    pl.when(has_low)(a_copy(False).start)

    def forward_own(l):
        for j in (1, 3, 2):
            y_arrival(4 - j, l).wait_recv()
            z_copy(0, l, j).start()

    loop(LAYERS, forward_own)

    def mode_id(at):
        side = (at >= SIDE).astype(jnp.int32)
        rest = at - SIDE * side
        block = sum((rest >= OWN * n).astype(jnp.int32) for n in (1, 2, 3))
        return rest + OWN * block + OWN * side

    nnz = values.shape[1]
    eye = lax.broadcasted_iota(jnp.int32, (nnz, nnz), 0) == lax.broadcasted_iota(jnp.int32, (nnz, nnz), 1)
    lane = lax.broadcasted_iota(jnp.int32, (nnz, 256), 1)
    slot = lane % 64
    col_id = jnp.where(slot < MODES, mode_id(slot), -1)
    low_part = lax.broadcasted_iota(jnp.int32, (8, 256), 1) >= 128

    def row_ids(count, start):
        at = lax.broadcasted_iota(jnp.int32, (count, nnz), 0)
        return jnp.where(at < min(count, MODES if count == MODES else SIDE), mode_id(at + start), -1)

    def build(tiles, start, target):
        ids = row_ids(tiles * 8, start)
        for k in range(TERMS):
            both = pairs[k]
            rows_here = jnp.sum(jnp.where(eye, both[:, 0:1], 0), axis=0, keepdims=True)
            left = jnp.where(ids == rows_here, values[k : k + 1, :], 0.0)
            right = jnp.where(col_id == both[:, 1:2], 1.0, 0.0)
            full = jnp.dot(left, right, precision=lax.Precision.HIGHEST, preferred_element_type=F32)
            for t in range(tiles):
                part = full[t * 8 : t * 8 + 8]
                high = part.astype(BF16).astype(F32)
                LF[t * 48 + k * 8 : t * 48 + k * 8 + 8, :] = jnp.where(low_part, part - high, high)
        target[...] = LF[0 : tiles * 48, :].astype(BF16)

    build(7, 0, L1)

    for hop in range(3):

        def forward(c, hop=hop):
            l, j = c // 4, lax.rem(c, 4)
            z_arrival(hop, l, j).wait_recv()
            z_copy(hop + 1, l, j).start()

        loop(16, forward)

        if hop == 0:
            build(4, zhi * SIDE, L2)
            own_a.wait()
            pl.when(y_low)(low_a.wait)
            pl.when(y_high)(high_a.wait)
            pl.when(has_low)(a_copy(True).wait_recv)
            pl.when(has_high)(a_copy(False).wait_recv)
            lanes = lax.broadcasted_iota(jnp.int32, (ROWS, 128), 1)

            def faces(i):
                k = i // LAYERS
                l = lax.rem(i, LAYERS)
                base = (k * 6 + l + 1) * HIGH_ROWS + 1
                a = A2[pl.ds(base, ROWS), :]
                near = (
                    A2[pl.ds(base - HIGH_ROWS, ROWS), :],
                    A2[pl.ds(base + HIGH_ROWS, ROWS), :],
                    A2[pl.ds(base - 1, ROWS), :],
                    A2[pl.ds(base + 1, ROWS), :],
                    jnp.where(lanes == 0, 0.0, pltpu.roll(a, 1, 1)),
                    jnp.where(lanes == 127, 0.0, pltpu.roll(a, 127, 1)),
                )
                for d in range(FACES):
                    FC2[pl.ds(l * (ROWS * 36) + d * 6 + k, ROWS, stride=36), :] = 0.5 * (a + near[d])

            loop(TERMS * LAYERS, faces)

    own_u.wait()

    def mix(matrix, a, b):
        u = jnp.concatenate([a, b], axis=1)
        u = jnp.concatenate([u, jnp.zeros((8, 256), F32)], axis=0)
        high = u.astype(BF16)
        low = (u - high.astype(F32)).astype(BF16)
        return jnp.dot(
            matrix[...], jnp.concatenate([high, low, high, low], axis=0), preferred_element_type=F32
        )

    def face_sum(row, d, v):
        total = None
        for k in range(TERMS):
            term = FC2[pl.ds(row * 36 + d * 6 + k, 1), :] * v[k]
            total = term if total is None else total + term
        return total

    lane8 = lax.broadcasted_iota(jnp.int32, (8, 128), 1)

    def place(l, r):
        return (l + 1) * HIGH_ROWS + r + 1

    def clear(i):
        O[i] = jnp.zeros((MODES, 128), F32)

    def own_pair(src, matrix, tiles, p):
        l = p // 6
        r = 2 * lax.rem(p, 6)
        q = 2 * p
        full = mix(
            matrix, src[pl.ds(q, MODES, stride=CELLS), :], src[pl.ds(q + 1, MODES, stride=CELLS), :]
        )
        for h in range(2):
            here = place(l, r + h)
            for t in range(tiles):
                v = [full[t * 48 + k * 8 : t * 48 + k * 8 + 8, h * 128 : h * 128 + 128] for k in range(TERMS)]
                xl, xr, yl, yr, zl, zr = [face_sum(q + h, d, v) for d in range(FACES)]
                zl_moved = jnp.where(lane8 == 127, 0.0, pltpu.roll(zl, 127, 1))
                zr_moved = jnp.where(lane8 == 0, 0.0, pltpu.roll(zr, 1, 1))
                tile = pl.ds(t * 8, 8)
                O[here, tile, :] += (xl + xr) + (yl + yr) + ((zl + zr) - (zl_moved + zr_moved))
                O[here - HIGH_ROWS, tile, :] -= xl
                O[here + HIGH_ROWS, tile, :] -= xr
                O[here - 1, tile, :] -= yl
                O[here + 1, tile, :] -= yr

    def halo_pair(src, stride, start, matrix, tiles, d, cells):
        full = mix(
            matrix, src[pl.ds(start, MODES, stride=stride), :], src[pl.ds(start + 1, MODES, stride=stride), :]
        )
        for h, (l, r) in enumerate(cells):
            for t in range(tiles):
                v = [full[t * 48 + k * 8 : t * 48 + k * 8 + 8, h * 128 : h * 128 + 128] for k in range(TERMS)]
                O[place(l, r), pl.ds(t * 8, 8), :] -= face_sum(l * ROWS + r, d, v)

    def halos_of(n, buf):
        def x(up):
            l, slot, s = (LAYERS - 1, 0, 1) if up else (0, 1, -1)
            return send(buf.at[:, l], HX.at[n, slot], h_send.at[n, int(up)], h_recv.at[n, int(up)], s_peer(s))

        def yy(up):
            r, slot, s = (ROWS - 1, 0, 1) if up else (0, 1, 3)
            return send(
                buf.at[:, :, r], HY.at[n, slot], h_send.at[n, 2 + int(up)], h_recv.at[n, 2 + int(up)], y_peer(s)
            )

        return x, yy

    def start_halos(n, buf):
        x, yy = halos_of(n, buf)
        pl.when(has_high)(x(True).start)
        pl.when(has_low)(x(False).start)
        pl.when(y_high)(yy(True).start)
        pl.when(y_low)(yy(False).start)

    def add_halos(n, buf, matrix, tiles):
        x, yy = halos_of(n, buf)
        pl.when(y_low)(yy(True).wait_recv)
        pl.when(y_high)(yy(False).wait_recv)
        for d, r in ((0, 0), (1, ROWS - 1)):

            def ybody(i, d=d, r=r):
                halo_pair(HY2[n][d], LAYERS, 2 * i, matrix, tiles, 2 + d, [(2 * i, r), (2 * i + 1, r)])

            loop(LAYERS // 2, ybody)
        pl.when(has_low)(x(True).wait_recv)
        pl.when(has_high)(x(False).wait_recv)
        for d, l in ((0, 0), (1, LAYERS - 1)):

            def xbody(i, d=d, l=l):
                halo_pair(HX2[n][d], ROWS, 2 * i, matrix, tiles, d, [(l, 2 * i), (l, 2 * i + 1)])

            loop(ROWS // 2, xbody)

    def end_halos(n, buf):
        x, yy = halos_of(n, buf)
        pl.when(has_high)(x(True).wait_send)
        pl.when(has_low)(x(False).wait_send)
        pl.when(y_high)(yy(True).wait_send)
        pl.when(y_low)(yy(False).wait_send)

    def out_copy(n, step):
        to = lax.rem(y + step, 4)
        if n == 0:
            src, dst = F.at[pl.ds(zhi * SIDE + to * OWN, OWN)], first_out
        else:
            src, dst = S.at[pl.ds(to * OWN, OWN)], second_out
        dst = dst.at[:, :, pl.ds(y * ROWS, ROWS)]
        if step == 0:
            return pltpu.make_async_copy(src, dst, loc.at[4 + n])
        return send(src, dst, o_send.at[n, step], o_recv.at[n, step], y_peer(step))

    def out_arrival(n, step):
        dst = (first_out, second_out)[n].at[:, :, pl.ds(lax.rem(y + 4 - step, 4) * ROWS, ROWS)]
        return send(F.at[pl.ds(0, OWN)], dst, o_send.at[n, step], o_recv.at[n, step], y_peer(step))

    loop(6 * HIGH_ROWS, clear)
    for l in range(LAYERS):

        def arrive(j, l=l):
            z_arrival(3, l, j).wait_recv()

        loop(4, arrive)
    start_halos(0, U)
    loop(24, functools.partial(own_pair, U2, L1, 7))
    add_halos(0, U, L1, 7)

    def finish_first(q):
        l = q // ROWS
        r = lax.rem(q, ROWS)
        F2[pl.ds(q, MODES, stride=CELLS), :] = O[place(l, r)]

    loop(CELLS, finish_first)
    start_halos(1, F)
    for step in range(4):
        out_copy(0, step).start()

    loop(6 * HIGH_ROWS, clear)
    loop(24, functools.partial(own_pair, F2, L2, 4))
    add_halos(1, F, L2, 4)

    def finish_second(q):
        l = q // ROWS
        r = lax.rem(q, ROWS)
        S2[pl.ds(q, 32, stride=CELLS), :] = O[place(l, r), 0:32, :]

    loop(CELLS, finish_second)
    for step in range(4):
        out_copy(1, step).start()

    end_halos(0, U)
    end_halos(1, F)
    for step in (1, 2, 3):
        for l in range(LAYERS):
            y_copy(step, l).wait_send()
    for hop in range(4):

        def drain(c, hop=hop):
            z_copy(hop, c // 4, lax.rem(c, 4)).wait_send()

        loop(16, drain)
    pl.when(has_high)(a_copy(True).wait_send)
    pl.when(has_low)(a_copy(False).wait_send)
    for n in range(2):
        out_copy(n, 0).wait()
        for step in (1, 2, 3):
            out_copy(n, step).wait_send()
            out_arrival(n, step).wait_recv()


def per_device(field, coeff, pairs, values):
    any_space = pl.BlockSpec(memory_space=pltpu.VMEM)
    out = jax.ShapeDtypeStruct((OWN, LAYERS, 48, 1, 128), F32)
    first, second = pl.pallas_call(
        kernel,
        out_shape=(out, out),
        in_specs=[any_space] * 4,
        out_specs=(any_space, any_space),
        scratch_shapes=[
            pltpu.VMEM((MODES, LAYERS, ROWS, 1, 128), F32),
            pltpu.VMEM((MODES, LAYERS, ROWS, 1, 128), F32),
            pltpu.VMEM((32, LAYERS, ROWS, 1, 128), F32),
            pltpu.VMEM((3, 16, OWN, ROWS, 1, 128), F32),
            pltpu.VMEM((2, 2, MODES, ROWS, 1, 128), F32),
            pltpu.VMEM((2, 2, MODES, LAYERS, 1, 128), F32),
            pltpu.VMEM((TERMS, 6, HIGH_ROWS, 1, 128), F32),
            pltpu.VMEM((CELLS * 36, 1, 128), F32),
            pltpu.VMEM((6 * HIGH_ROWS, MODES, 128), F32),
            pltpu.VMEM((336, 256), F32),
            pltpu.VMEM((336, 256), BF16),
            pltpu.VMEM((192, 256), BF16),
            pltpu.SemaphoreType.DMA((4, LAYERS)),
            pltpu.SemaphoreType.DMA((4, LAYERS)),
            pltpu.SemaphoreType.DMA((4, 16)),
            pltpu.SemaphoreType.DMA((4, 16)),
            pltpu.SemaphoreType.DMA((2,)),
            pltpu.SemaphoreType.DMA((2,)),
            pltpu.SemaphoreType.DMA((2, 4)),
            pltpu.SemaphoreType.DMA((2, 4)),
            pltpu.SemaphoreType.DMA((2, 4)),
            pltpu.SemaphoreType.DMA((2, 4)),
            pltpu.SemaphoreType.DMA((8,)),
        ],
        compiler_params=pltpu.CompilerParams(
            collective_id=0, has_side_effects=True, vmem_limit_bytes=48 << 20
        ),
    )(
        field.reshape(OWN, LAYERS, 48, 1, 128),
        coeff.reshape(TERMS, LAYERS, 48, 1, 128),
        pairs,
        values,
    )
    return first.reshape(field.shape), second.reshape(field.shape)


def solution(mesh):
    in_specs = (P("mode", "space", None, None), P(None, "space", None, None), P(), P())
    out_specs = (P("mode", "space", None, None), P("mode", "space", None, None))
    return jax.shard_map(
        per_device, mesh=mesh, in_specs=in_specs, out_specs=out_specs, check_vma=False
    )
```

```python
import functools

import jax
import jax.numpy as jnp
from jax import lax
from jax.experimental import pallas as pl
from jax.experimental.pallas import tpu as pltpu
from jax.sharding import PartitionSpec as P

MESH = pl.DeviceIdType.MESH
F32 = jnp.float32
BF16 = jnp.bfloat16

TERMS = 6
OWN = 7
SIDE = 28
MODES = 56
LAYERS = 4
ROWS = 12
CELLS = LAYERS * ROWS
FACES = 6
HIGH_ROWS = ROWS + 2
NR = 2
NC = ROWS // NR
AHEAD = 2


def kernel(
    field,
    coeff,
    pairs,
    values,
    first_out,
    second_out,
    U,
    F,
    S,
    XB1,
    XB2,
    YB1,
    YB2,
    A,
    FC,
    O1,
    O2,
    LF,
    L1,
    L2,
    y_send,
    y_recv,
    z_send,
    z_recv,
    c_send,
    c_recv,
    x_send,
    x_recv,
    b_send,
    b_recv,
    o_send,
    o_recv,
    loc,
    o_loc,
):
    space = lax.axis_index("space")
    mode = lax.axis_index("mode")
    y = mode // 2
    zhi = mode % 2

    def y_peer(step):
        return (space, lax.rem(y + step, 4) * 2 + zhi)

    partner = (space, y * 2 + 1 - zhi)

    def s_peer(step):
        return (space + step, mode)

    def send(src, dst, ss, rs, dev):
        return pltpu.make_async_remote_copy(
            src_ref=src, dst_ref=dst, send_sem=ss, recv_sem=rs, device_id=dev, device_id_type=MESH
        )

    def loop(n, body):
        def step(i, carry):
            body(i)
            return carry

        lax.fori_loop(0, n, step, 0)

    has_low = space > 0
    has_high = space < 31
    y_low = y > 0
    y_high = y < 3

    def chunk_row(at, c):
        return jnp.where(at % 2 == 0, c * NR, ROWS - (c + 1) * NR)

    U2 = U.reshape(NC * MODES * LAYERS * NR, 128)
    F2 = F.reshape(NC * MODES * LAYERS * NR, 128)
    S2 = S.reshape(NC * 32 * LAYERS * NR, 128)
    A2 = A.reshape(TERMS * 6 * HIGH_ROWS, 128)
    FC2 = FC.reshape(CELLS * 36, 128)

    A2[...] = jnp.zeros(A2.shape, F32)

    barrier = pltpu.get_barrier_semaphore()
    for step in (1, 2, 3):
        pl.semaphore_signal(barrier, inc=1, device_id=y_peer(step), device_id_type=MESH)
    pl.semaphore_signal(barrier, inc=1, device_id=partner, device_id_type=MESH)

    @pl.when(has_low)
    def _():
        pl.semaphore_signal(barrier, inc=1, device_id=s_peer(-1), device_id_type=MESH)

    @pl.when(has_high)
    def _():
        pl.semaphore_signal(barrier, inc=1, device_id=s_peer(1), device_id_type=MESH)

    pl.semaphore_wait(barrier, 4 + has_low.astype(jnp.int32) + has_high.astype(jnp.int32))

    def y_copy(step, c):
        to = lax.rem(y + step, 4)
        return send(
            field.at[:, :, pl.ds(to * ROWS + chunk_row(to, c), NR)],
            U.at[c, pl.ds(zhi * SIDE + y * OWN, OWN)],
            y_send.at[step, c],
            y_recv.at[step, c],
            y_peer(step),
        )

    def y_arrival(step, c):
        src = lax.rem(y + 4 - step, 4)
        return send(
            field.at[:, :, pl.ds(0, NR)],
            U.at[c, pl.ds(zhi * SIDE + src * OWN, OWN)],
            y_send.at[step, c],
            y_recv.at[step, c],
            y_peer(step),
        )

    def own_rows(c):
        return field.at[:, :, pl.ds(y * ROWS + chunk_row(y, c), NR)]

    def z_copy(c, j):
        at = pl.ds(zhi * SIDE + lax.rem(y + j, 4) * OWN, OWN)
        src = own_rows(c) if j == 0 else U.at[c, at]
        return send(src, U.at[c, at], z_send.at[c, j], z_recv.at[c, j], partner)

    def z_arrival(c, j):
        at = pl.ds((1 - zhi) * SIDE + lax.rem(y + j, 4) * OWN, OWN)
        return send(U.at[c, at], U.at[c, at], z_send.at[c, j], z_recv.at[c, j], partner)

    for c in range(AHEAD):
        z_copy(c, 0).start()

    def start_y(c):
        for step in (1, 3, 2):
            y_copy(step, c).start()

    loop(NC, start_y)

    def own_copy(c):
        return pltpu.make_async_copy(own_rows(c), U.at[c, pl.ds(zhi * SIDE + y * OWN, OWN)], loc.at[3 + c])

    loop(NC, lambda c: own_copy(c).start())

    own_a = pltpu.make_async_copy(
        coeff.at[:, :, pl.ds(y * ROWS, ROWS)], A.at[:, pl.ds(1, LAYERS), pl.ds(1, ROWS)], loc.at[0]
    )
    low_a = pltpu.make_async_copy(
        coeff.at[:, :, pl.ds(jnp.maximum(y * ROWS - 1, 0), 1)],
        A.at[:, pl.ds(1, LAYERS), pl.ds(0, 1)],
        loc.at[1],
    )
    high_a = pltpu.make_async_copy(
        coeff.at[:, :, pl.ds(jnp.minimum(y * ROWS + ROWS, 47), 1)],
        A.at[:, pl.ds(1, LAYERS), pl.ds(ROWS + 1, 1)],
        loc.at[2],
    )

    def a_copy(up):
        l, slot, s = (LAYERS - 1, 0, 1) if up else (0, LAYERS + 1, -1)
        return send(
            coeff.at[:, l, pl.ds(y * ROWS, ROWS)],
            A.at[:, slot, pl.ds(1, ROWS)],
            c_send.at[int(up)],
            c_recv.at[int(up)],
            s_peer(s),
        )

    own_a.start()
    pl.when(y_low)(low_a.start)
    pl.when(y_high)(high_a.start)
    pl.when(has_high)(a_copy(True).start)
    pl.when(has_low)(a_copy(False).start)

    def y_to_z(c):
        for j in (1, 3, 2):
            y_arrival(4 - j, c).wait_recv()
            z_copy(c, j).start()

    for c in range(AHEAD):
        y_to_z(c)

    def mode_id(at):
        side = (at >= SIDE).astype(jnp.int32)
        rest = at - SIDE * side
        block = sum((rest >= OWN * n).astype(jnp.int32) for n in (1, 2, 3))
        return rest + OWN * block + OWN * side

    nnz = values.shape[1]
    eye = lax.broadcasted_iota(jnp.int32, (nnz, nnz), 0) == lax.broadcasted_iota(jnp.int32, (nnz, nnz), 1)
    slot = lax.broadcasted_iota(jnp.int32, (nnz, 256), 1) % 64
    col_id = jnp.where(slot < MODES, mode_id(slot), -1)
    low_part = lax.broadcasted_iota(jnp.int32, (8, 256), 1) >= 128

    def build(tiles, start, count, target):
        at = lax.broadcasted_iota(jnp.int32, (tiles * 8, nnz), 0)
        ids = jnp.where(at < count, mode_id(at + start), -1)

        def term(k):
            both = pairs[k]
            cols = jnp.sum(jnp.where(eye, both[1:2, :], 0), axis=1, keepdims=True)
            left = jnp.where(ids == both[0:1, :], values[pl.ds(k, 1), :], 0.0)
            right = jnp.where(col_id == cols, 1.0, 0.0)
            full = jnp.dot(left, right, precision=lax.Precision.HIGHEST, preferred_element_type=F32)
            for t in range(tiles):
                part = full[t * 8 : t * 8 + 8]
                high = part.astype(BF16).astype(F32)
                LF[pl.ds(pl.multiple_of(t * 48 + k * 8, 8), 8), :] = jnp.where(low_part, part - high, high)

        loop(TERMS, term)
        target[...] = LF[0 : tiles * 48, :].astype(BF16)

    build(7, 0, MODES, L1)
    build(4, zhi * SIDE, SIDE, L2)

    own_a.wait()
    pl.when(y_low)(low_a.wait)
    pl.when(y_high)(high_a.wait)
    pl.when(has_low)(a_copy(True).wait_recv)
    pl.when(has_high)(a_copy(False).wait_recv)
    lanes = lax.broadcasted_iota(jnp.int32, (ROWS, 128), 1)

    def faces(i):
        k = i // LAYERS
        l = lax.rem(i, LAYERS)
        base = (k * 6 + l + 1) * HIGH_ROWS + 1
        a = A2[pl.ds(base, ROWS), :]
        near = (
            A2[pl.ds(base - HIGH_ROWS, ROWS), :],
            A2[pl.ds(base + HIGH_ROWS, ROWS), :],
            A2[pl.ds(base - 1, ROWS), :],
            A2[pl.ds(base + 1, ROWS), :],
            jnp.where(lanes == 0, 0.0, pltpu.roll(a, 1, 1)),
            jnp.where(lanes == 127, 0.0, pltpu.roll(a, 127, 1)),
        )
        for d in range(FACES):
            FC2[pl.ds(l * (ROWS * 36) + d * 6 + k, ROWS, stride=36), :] = 0.5 * (a + near[d])

    loop(TERMS * LAYERS, faces)

    def clear(i):
        l = i // HIGH_ROWS
        r = lax.rem(i, HIGH_ROWS)
        O1[l, r] = jnp.zeros((MODES, 128), F32)
        O2[l, r] = jnp.zeros((32, 128), F32)

    loop(6 * HIGH_ROWS, clear)
    loop(NC, lambda c: own_copy(c).wait())

    def mix(matrix, a, b):
        u = jnp.concatenate([a, b], axis=1)
        u = jnp.concatenate([u, jnp.zeros((8, 256), F32)], axis=0)
        high = u.astype(BF16)
        low = (u - high.astype(F32)).astype(BF16)
        return jnp.dot(
            matrix[...], jnp.concatenate([high, low, high, low], axis=0), preferred_element_type=F32
        )

    def face_sum(row, d, v):
        total = None
        for k in range(TERMS):
            term = FC2[pl.ds(row * 36 + d * 6 + k, 1), :] * v[k]
            total = term if total is None else total + term
        return total

    lane8 = lax.broadcasted_iota(jnp.int32, (8, 128), 1)

    def apply_chunk(src, O, matrix, tiles, c):
        def pair(p):
            i = p // 2
            l = 2 * lax.rem(p, 2)
            r = chunk_row(y, c) + i
            base = c * (MODES * LAYERS * NR) + l * NR + i
            full = mix(
                matrix,
                src[pl.ds(base, MODES, stride=LAYERS * NR), :],
                src[pl.ds(base + NR, MODES, stride=LAYERS * NR), :],
            )
            for h in range(2):
                at_l, at_r, row = l + 1 + h, r + 1, (l + h) * ROWS + r
                for t in range(tiles):
                    v = [full[t * 48 + k * 8 : t * 48 + k * 8 + 8, h * 128 : h * 128 + 128] for k in range(TERMS)]
                    xl, xr, yl, yr, zl, zr = [face_sum(row, d, v) for d in range(FACES)]
                    zl_moved = jnp.where(lane8 == 127, 0.0, pltpu.roll(zl, 127, 1))
                    zr_moved = jnp.where(lane8 == 0, 0.0, pltpu.roll(zr, 1, 1))
                    tile = pl.ds(t * 8, 8)
                    O[at_l, at_r, tile, :] += (xl + xr) + (yl + yr) + ((zl + zr) - (zl_moved + zr_moved))
                    O[at_l - 1, at_r, tile, :] -= xl
                    O[at_l + 1, at_r, tile, :] -= xr
                    O[at_l, at_r - 1, tile, :] -= yl
                    O[at_l, at_r + 1, tile, :] -= yr

        loop(2 * NR, pair)

    def borders(n):
        O, XB, YB, count = ((O1, XB1, YB1, MODES), (O2, XB2, YB2, SIDE))[n]
        some = pl.ds(0, count)

        def x(up, c):
            l, slot, s = (LAYERS + 1, 0, 1) if up else (0, 1, -1)
            return send(
                O.at[l, pl.ds(chunk_row(y, c) + 1, NR), some],
                XB.at[slot, c, :, some],
                x_send.at[n, int(up), c],
                x_recv.at[n, int(up), c],
                s_peer(s),
            )

        def yy(up):
            r, slot, s = (ROWS + 1, 0, 1) if up else (0, 1, 3)
            return send(
                O.at[pl.ds(1, LAYERS), r, some],
                YB.at[slot, :, some],
                b_send.at[n, int(up)],
                b_recv.at[n, int(up)],
                y_peer(s),
            )

        return x, yy

    def early_up(c):
        return jnp.where(y % 2 == 0, c == NC - 1, c == 0)

    def early_down(c):
        return jnp.where(y % 2 == 0, c == 0, c == NC - 1)

    def send_borders(n, c):
        x, yy = borders(n)
        pl.when(has_high)(x(True, c).start)
        pl.when(has_low)(x(False, c).start)
        pl.when(jnp.logical_and(y_high, early_up(c)))(yy(True).start)
        pl.when(jnp.logical_and(y_low, early_down(c)))(yy(False).start)

    def add_borders(n, c):
        x, yy = borders(n)
        O, XB, YB, modes = ((O1, XB1, YB1, MODES), (O2, XB2, YB2, 32))[n]
        r = chunk_row(y, c) + 1

        @pl.when(has_low)
        def _():
            x(True, c).wait_recv()
            for i in range(NR):
                O[1, r + i] += XB[0, c, i]

        @pl.when(has_high)
        def _():
            x(False, c).wait_recv()
            for i in range(NR):
                O[LAYERS, r + i] += XB[1, c, i]

        @pl.when(jnp.logical_and(y_low, early_down(c)))
        def _():
            yy(True).wait_recv()
            for l in range(LAYERS):
                O[l + 1, 1] += YB[0, l]

        @pl.when(jnp.logical_and(y_high, early_up(c)))
        def _():
            yy(False).wait_recv()
            for l in range(LAYERS):
                O[l + 1, ROWS] += YB[1, l]

    def out_copy(n, step, c):
        to = lax.rem(y + step, 4)
        if n == 0:
            src, dst = F.at[c, pl.ds(zhi * SIDE + to * OWN, OWN)], first_out
        else:
            src, dst = S.at[c, pl.ds(to * OWN, OWN)], second_out
        dst = dst.at[:, :, pl.ds(y * ROWS + chunk_row(y, c), NR)]
        if step == 0:
            return pltpu.make_async_copy(src, dst, o_loc.at[n, c])
        return send(src, dst, o_send.at[n, step, c], o_recv.at[n, step, c], y_peer(step))

    def out_arrival(n, step, c):
        src = lax.rem(y + 4 - step, 4)
        dst = (first_out, second_out)[n].at[:, :, pl.ds(src * ROWS + chunk_row(src, c), NR)]
        return send(F.at[0, pl.ds(0, OWN)], dst, o_send.at[n, step, c], o_recv.at[n, step, c], y_peer(step))

    def finish(n, c):
        add_borders(n, c)
        O, to, modes = ((O1, F2, MODES), (O2, S2, 32))[n]
        r = chunk_row(y, c) + 1
        for i in range(NR):
            for l in range(LAYERS):
                to[pl.ds(c * (modes * LAYERS * NR) + l * NR + i, modes, stride=LAYERS * NR), :] = O[l + 1, r + i]
        for step in (2, 1, 3, 0):
            out_copy(n, step, c).start()

    def stage(c):
        @pl.when(c < NC)
        def _():
            for j in range(4):
                z_arrival(c, j).wait_recv()
            apply_chunk(U2, O1, L1, 7, c)
            send_borders(0, c)

        @pl.when(c + AHEAD < NC)
        def _():
            z_copy(c + AHEAD, 0).start()
            y_to_z(c + AHEAD)

        @pl.when(jnp.logical_and(c >= 1, c <= NC))
        def _():
            finish(0, c - 1)
            apply_chunk(F2, O2, L2, 4, c - 1)
            send_borders(1, c - 1)

        @pl.when(c >= 2)
        def _():
            finish(1, c - 2)

    loop(NC + 2, stage)

    def drain(c):
        for step in (1, 2, 3):
            y_copy(step, c).wait_send()
        for j in range(4):
            z_copy(c, j).wait_send()
        for n in range(2):
            x, _ = borders(n)
            pl.when(has_high)(x(True, c).wait_send)
            pl.when(has_low)(x(False, c).wait_send)
            out_copy(n, 0, c).wait()
            for step in (1, 2, 3):
                out_copy(n, step, c).wait_send()
                out_arrival(n, step, c).wait_recv()

    loop(NC, drain)
    for n in range(2):
        _, yy = borders(n)
        pl.when(y_high)(yy(True).wait_send)
        pl.when(y_low)(yy(False).wait_send)
    pl.when(has_high)(a_copy(True).wait_send)
    pl.when(has_low)(a_copy(False).wait_send)


def per_device(field, coeff, pairs, values):
    vmem = pl.BlockSpec(memory_space=pltpu.VMEM)
    hbm = pl.BlockSpec(memory_space=pl.ANY)
    out = jax.ShapeDtypeStruct((OWN, LAYERS, 48, 1, 128), F32)
    sem = pltpu.SemaphoreType.DMA
    first, second = pl.pallas_call(
        kernel,
        out_shape=(out, out),
        in_specs=[hbm, hbm, vmem, vmem],
        out_specs=(vmem, vmem),
        scratch_shapes=[
            pltpu.VMEM((NC, MODES, LAYERS, NR, 1, 128), F32),
            pltpu.VMEM((NC, MODES, LAYERS, NR, 1, 128), F32),
            pltpu.VMEM((NC, 32, LAYERS, NR, 1, 128), F32),
            pltpu.VMEM((2, NC, NR, MODES, 128), F32),
            pltpu.VMEM((2, NC, NR, 32, 128), F32),
            pltpu.VMEM((2, LAYERS, MODES, 128), F32),
            pltpu.VMEM((2, LAYERS, 32, 128), F32),
            pltpu.VMEM((TERMS, 6, HIGH_ROWS, 1, 128), F32),
            pltpu.VMEM((CELLS * 36, 1, 128), F32),
            pltpu.VMEM((6, HIGH_ROWS, MODES, 128), F32),
            pltpu.VMEM((6, HIGH_ROWS, 32, 128), F32),
            pltpu.VMEM((336, 256), F32),
            pltpu.VMEM((336, 256), BF16),
            pltpu.VMEM((192, 256), BF16),
            sem((4, NC)),
            sem((4, NC)),
            sem((NC, 4)),
            sem((NC, 4)),
            sem((2,)),
            sem((2,)),
            sem((2, 2, NC)),
            sem((2, 2, NC)),
            sem((2, 2)),
            sem((2, 2)),
            sem((2, 4, NC)),
            sem((2, 4, NC)),
            sem((3 + NC,)),
            sem((2, NC)),
        ],
        compiler_params=pltpu.CompilerParams(
            collective_id=0, has_side_effects=True, vmem_limit_bytes=48 << 20
        ),
    )(
        field.reshape(OWN, LAYERS, 48, 1, 128),
        coeff.reshape(TERMS, LAYERS, 48, 1, 128),
        jnp.transpose(pairs, (0, 2, 1)),
        values,
    )
    return first.reshape(field.shape), second.reshape(field.shape)


def solution(mesh):
    in_specs = (P("mode", "space", None, None), P(None, "space", None, None), P(), P())
    out_specs = (P("mode", "space", None, None), P("mode", "space", None, None))
    return jax.shard_map(
        per_device, mesh=mesh, in_specs=in_specs, out_specs=out_specs, check_vma=False
    )
```

```python
import functools

import jax
import jax.numpy as jnp
from jax import lax
from jax.experimental import pallas as pl
from jax.experimental.pallas import tpu as pltpu
from jax.sharding import PartitionSpec as P

MESH = pl.DeviceIdType.MESH
F32 = jnp.float32
BF16 = jnp.bfloat16

TERMS = 6
OWN = 7
SIDE = 28
MODES = 56
LAYERS = 4
ROWS = 12
CELLS = LAYERS * ROWS
FACES = 6
HIGH_ROWS = ROWS + 2
NR = 2
NC = ROWS // NR
AHEAD = 3
LAG = 2


def kernel(
    field,
    coeff,
    pairs,
    values,
    first_out,
    second_out,
    U,
    F,
    S,
    XB1,
    XB2,
    YB1,
    YB2,
    A,
    FC,
    O1,
    O2,
    LF,
    L1,
    L2,
    y_send,
    y_recv,
    z_send,
    z_recv,
    c_send,
    c_recv,
    x_send,
    x_recv,
    b_send,
    b_recv,
    o_send,
    o_recv,
    loc,
    o_loc,
):
    space = lax.axis_index("space")
    mode = lax.axis_index("mode")
    y = mode // 2
    zhi = mode % 2

    def y_peer(step):
        return (space, lax.rem(y + step, 4) * 2 + zhi)

    partner = (space, y * 2 + 1 - zhi)

    def s_peer(step):
        return (space + step, mode)

    at_end = {1: space % 8 == 7, -1: space % 8 == 0}

    def near_peer(step):
        return (space + step, jnp.where(at_end[step], y * 2 + 1 - zhi, mode))

    def send(src, dst, ss, rs, dev):
        return pltpu.make_async_remote_copy(
            src_ref=src, dst_ref=dst, send_sem=ss, recv_sem=rs, device_id=dev, device_id_type=MESH
        )

    def loop(n, body):
        def step(i, carry):
            body(i)
            return carry

        lax.fori_loop(0, n, step, 0)

    has_low = space > 0
    has_high = space < 31
    y_low = y > 0
    y_high = y < 3

    def chunk_row(c):
        return NR * jnp.where(c % 2 == 0, c // 2, NC - 1 - c // 2)

    U2 = U.reshape(NC * MODES * LAYERS * NR, 128)
    F2 = F.reshape(NC * MODES * LAYERS * NR, 128)
    S2 = S.reshape(NC * 32 * LAYERS * NR, 128)
    A2 = A.reshape(TERMS * 6 * HIGH_ROWS, 128)
    FC2 = FC.reshape(CELLS * 36, 128)

    A2[...] = jnp.zeros(A2.shape, F32)

    barrier = pltpu.get_barrier_semaphore()
    for step in (1, 2, 3):
        pl.semaphore_signal(barrier, inc=1, device_id=y_peer(step), device_id_type=MESH)
    pl.semaphore_signal(barrier, inc=1, device_id=partner, device_id_type=MESH)

    expected = jnp.int32(4)
    for present, step in ((has_low, -1), (has_high, 1)):
        turned = jnp.logical_and(present, at_end[step])

        @pl.when(present)
        def _(step=step):
            pl.semaphore_signal(barrier, inc=1, device_id=s_peer(step), device_id_type=MESH)

        @pl.when(turned)
        def _(step=step):
            pl.semaphore_signal(barrier, inc=1, device_id=near_peer(step), device_id_type=MESH)

        expected = expected + present.astype(jnp.int32) + turned.astype(jnp.int32)
    pl.semaphore_wait(barrier, expected)

    def y_copy(step, c):
        to = lax.rem(y + step, 4)
        return send(
            field.at[:, :, pl.ds(to * ROWS + chunk_row(c), NR)],
            U.at[c, pl.ds(zhi * SIDE + y * OWN, OWN)],
            y_send.at[0],
            y_recv.at[c],
            y_peer(step),
        )

    def wait_y(c):
        three = U.at[c, pl.ds(0, 3 * OWN)]
        send(three, three, y_send.at[0], y_recv.at[c], partner).wait_recv()

    def own_rows(c):
        return field.at[:, :, pl.ds(y * ROWS + chunk_row(c), NR)]

    def z_copy(c, j):
        at = pl.ds(zhi * SIDE + lax.rem(y + j, 4) * OWN, OWN)
        src = own_rows(c) if j == 0 else U.at[c, at]
        return send(src, U.at[c, at], z_send.at[0], z_recv.at[c], partner)

    def wait_z(c):
        side = U.at[c, pl.ds((1 - zhi) * SIDE, SIDE)]
        send(side, side, z_send.at[0], z_recv.at[c], partner).wait_recv()

    def own_copy(c):
        return pltpu.make_async_copy(own_rows(c), U.at[c, pl.ds(zhi * SIDE + y * OWN, OWN)], loc.at[3])

    def start_field(c):
        for step in (1, 3, 2):
            y_copy(step, c).start()
        z_copy(c, 0).start()

    loop(NC, start_field)

    own_a = pltpu.make_async_copy(
        coeff.at[:, :, pl.ds(y * ROWS, ROWS)], A.at[:, pl.ds(1, LAYERS), pl.ds(1, ROWS)], loc.at[0]
    )
    low_a = pltpu.make_async_copy(
        coeff.at[:, :, pl.ds(jnp.maximum(y * ROWS - 1, 0), 1)],
        A.at[:, pl.ds(1, LAYERS), pl.ds(0, 1)],
        loc.at[1],
    )
    high_a = pltpu.make_async_copy(
        coeff.at[:, :, pl.ds(jnp.minimum(y * ROWS + ROWS, 47), 1)],
        A.at[:, pl.ds(1, LAYERS), pl.ds(ROWS + 1, 1)],
        loc.at[2],
    )

    def a_copy(up):
        l, slot, s = (LAYERS - 1, 0, 1) if up else (0, LAYERS + 1, -1)
        return send(
            coeff.at[:, l, pl.ds(y * ROWS, ROWS)],
            A.at[:, slot, pl.ds(1, ROWS)],
            c_send.at[int(up)],
            c_recv.at[int(up)],
            near_peer(s),
        )

    own_a.start()
    pl.when(y_low)(low_a.start)
    pl.when(y_high)(high_a.start)
    pl.when(has_high)(a_copy(True).start)
    pl.when(has_low)(a_copy(False).start)

    loop(NC, lambda c: own_copy(c).start())

    def y_to_z(c):
        wait_y(c)
        for j in (1, 2, 3):
            z_copy(c, j).start()

    loop(AHEAD, y_to_z)

    def mode_id(at):
        side = (at >= SIDE).astype(jnp.int32)
        rest = at - SIDE * side
        block = sum((rest >= OWN * n).astype(jnp.int32) for n in (1, 2, 3))
        return rest + OWN * block + OWN * side

    nnz = values.shape[1]
    eye = lax.broadcasted_iota(jnp.int32, (nnz, nnz), 0) == lax.broadcasted_iota(jnp.int32, (nnz, nnz), 1)
    slot = lax.broadcasted_iota(jnp.int32, (nnz, 256), 1) % 64
    col_id = jnp.where(slot < MODES, mode_id(slot), -1)
    low_part = lax.broadcasted_iota(jnp.int32, (8, 256), 1) >= 128

    def build(tiles, start, count, target):
        at = lax.broadcasted_iota(jnp.int32, (tiles * 8, nnz), 0)
        ids = jnp.where(at < count, mode_id(at + start), -1)

        def term(k):
            both = pairs[k]
            cols = jnp.sum(jnp.where(eye, both[1:2, :], 0), axis=1, keepdims=True)
            left = jnp.where(ids == both[0:1, :], values[pl.ds(k, 1), :], 0.0)
            right = jnp.where(col_id == cols, 1.0, 0.0)
            full = jnp.dot(left, right, precision=lax.Precision.HIGHEST, preferred_element_type=F32)
            for t in range(tiles):
                part = full[t * 8 : t * 8 + 8]
                high = part.astype(BF16).astype(F32)
                LF[pl.ds(pl.multiple_of(t * 48 + k * 8, 8), 8), :] = jnp.where(low_part, part - high, high)

        loop(TERMS, term)
        target[...] = LF[0 : tiles * 48, :].astype(BF16)

    build(7, 0, MODES, L1)
    build(4, zhi * SIDE, SIDE, L2)

    own_a.wait()
    pl.when(y_low)(low_a.wait)
    pl.when(y_high)(high_a.wait)
    pl.when(has_low)(a_copy(True).wait_recv)
    pl.when(has_high)(a_copy(False).wait_recv)
    lanes = lax.broadcasted_iota(jnp.int32, (ROWS, 128), 1)

    def faces(i):
        k = i // LAYERS
        l = lax.rem(i, LAYERS)
        base = (k * 6 + l + 1) * HIGH_ROWS + 1
        a = A2[pl.ds(base, ROWS), :]
        near = (
            A2[pl.ds(base - HIGH_ROWS, ROWS), :],
            A2[pl.ds(base + HIGH_ROWS, ROWS), :],
            A2[pl.ds(base - 1, ROWS), :],
            A2[pl.ds(base + 1, ROWS), :],
            jnp.where(lanes == 0, 0.0, pltpu.roll(a, 1, 1)),
            jnp.where(lanes == 127, 0.0, pltpu.roll(a, 127, 1)),
        )
        for d in range(FACES):
            FC2[pl.ds(l * (ROWS * 36) + d * 6 + k, ROWS, stride=36), :] = 0.5 * (a + near[d])

    loop(TERMS * LAYERS, faces)

    def clear(i):
        l = i // HIGH_ROWS
        r = lax.rem(i, HIGH_ROWS)
        O1[l, r] = jnp.zeros((MODES, 128), F32)
        O2[l, r] = jnp.zeros((32, 128), F32)

    loop(6 * HIGH_ROWS, clear)
    own = U.at[:, pl.ds(0, OWN)]
    pltpu.make_async_copy(own, own, loc.at[3]).wait()

    def mix(matrix, a, b):
        u = jnp.concatenate([a, b], axis=1)
        u = jnp.concatenate([u, jnp.zeros((8, 256), F32)], axis=0)
        high = u.astype(BF16)
        low = (u - high.astype(F32)).astype(BF16)
        return jnp.dot(
            matrix[...], jnp.concatenate([high, low, high, low], axis=0), preferred_element_type=F32
        )

    def face_sum(row, d, v):
        total = None
        for k in range(TERMS):
            term = FC2[pl.ds(row * 36 + d * 6 + k, 1), :] * v[k]
            total = term if total is None else total + term
        return total

    lane8 = lax.broadcasted_iota(jnp.int32, (8, 128), 1)

    def apply_chunk(src, O, matrix, tiles, c):
        def pair(p):
            i = p // 2
            l = 2 * lax.rem(p, 2)
            r = chunk_row(c) + i
            base = c * (MODES * LAYERS * NR) + l * NR + i
            full = mix(
                matrix,
                src[pl.ds(base, MODES, stride=LAYERS * NR), :],
                src[pl.ds(base + NR, MODES, stride=LAYERS * NR), :],
            )
            for h in range(2):
                at_l, at_r, row = l + 1 + h, r + 1, (l + h) * ROWS + r
                for t in range(tiles):
                    v = [full[t * 48 + k * 8 : t * 48 + k * 8 + 8, h * 128 : h * 128 + 128] for k in range(TERMS)]
                    xl, xr, yl, yr, zl, zr = [face_sum(row, d, v) for d in range(FACES)]
                    zl_moved = jnp.where(lane8 == 127, 0.0, pltpu.roll(zl, 127, 1))
                    zr_moved = jnp.where(lane8 == 0, 0.0, pltpu.roll(zr, 1, 1))
                    tile = pl.ds(t * 8, 8)
                    O[at_l, at_r, tile, :] += (xl + xr) + (yl + yr) + ((zl + zr) - (zl_moved + zr_moved))
                    O[at_l - 1, at_r, tile, :] -= xl
                    O[at_l + 1, at_r, tile, :] -= xr
                    O[at_l, at_r - 1, tile, :] -= yl
                    O[at_l, at_r + 1, tile, :] -= yr

        loop(2 * NR, pair)

    def borders(n):
        O, XB, YB, count = ((O1, XB1, YB1, MODES), (O2, XB2, YB2, SIDE))[n]
        some = pl.ds(0, count)

        def x(up, c):
            l, slot, s = (LAYERS + 1, 0, 1) if up else (0, 1, -1)
            return send(
                O.at[l, pl.ds(chunk_row(c) + 1, NR), some],
                XB.at[slot, c, :, some],
                x_send.at[n, int(up)],
                x_recv.at[n, int(up), c],
                (near_peer, s_peer)[n](s),
            )

        def yy(up):
            r, slot, s = (ROWS + 1, 0, 1) if up else (0, 1, 3)
            return send(
                O.at[pl.ds(1, LAYERS), r, some],
                YB.at[slot, :, some],
                b_send.at[n, int(up)],
                b_recv.at[n, int(up)],
                y_peer(s),
            )

        return x, yy

    def is_top(c):
        return c == 1

    def is_bottom(c):
        return c == 0

    def send_borders(n, c):
        x, yy = borders(n)
        pl.when(has_high)(x(True, c).start)
        pl.when(has_low)(x(False, c).start)
        pl.when(jnp.logical_and(y_high, is_top(c)))(yy(True).start)
        pl.when(jnp.logical_and(y_low, is_bottom(c)))(yy(False).start)

    def add_borders(n, c):
        x, yy = borders(n)
        O, XB, YB, modes = ((O1, XB1, YB1, MODES), (O2, XB2, YB2, 32))[n]
        r = chunk_row(c) + 1

        @pl.when(has_low)
        def _():
            x(True, c).wait_recv()
            for i in range(NR):
                O[1, r + i] += XB[0, c, i]

        @pl.when(has_high)
        def _():
            x(False, c).wait_recv()
            for i in range(NR):
                O[LAYERS, r + i] += XB[1, c, i]

        @pl.when(jnp.logical_and(y_low, is_bottom(c)))
        def _():
            yy(True).wait_recv()
            for l in range(LAYERS):
                O[l + 1, 1] += YB[0, l]

        @pl.when(jnp.logical_and(y_high, is_top(c)))
        def _():
            yy(False).wait_recv()
            for l in range(LAYERS):
                O[l + 1, ROWS] += YB[1, l]

    def out_copy(n, step, c):
        to = lax.rem(y + step, 4)
        if n == 0:
            src, dst = F.at[c, pl.ds(zhi * SIDE + to * OWN, OWN)], first_out
        else:
            src, dst = S.at[c, pl.ds(to * OWN, OWN)], second_out
        dst = dst.at[:, :, pl.ds(y * ROWS + chunk_row(c), NR)]
        if step == 0:
            return pltpu.make_async_copy(src, dst, o_loc.at[n])
        return send(src, dst, o_send.at[n], o_recv.at[n], y_peer(step))

    def finish(n, c):
        add_borders(n, c)
        O, to, modes = ((O1, F2, MODES), (O2, S2, 32))[n]
        r = chunk_row(c) + 1
        for i in range(NR):
            for l in range(LAYERS):
                to[pl.ds(c * (modes * LAYERS * NR) + l * NR + i, modes, stride=LAYERS * NR), :] = O[l + 1, r + i]
        for step in (2, 1, 3, 0):
            out_copy(n, step, c).start()

    def stage(c):
        @pl.when(c < NC)
        def _():
            wait_z(c)
            apply_chunk(U2, O1, L1, 7, c)
            send_borders(0, c)

        @pl.when(c + AHEAD < NC)
        def _():
            y_to_z(c + AHEAD)

        @pl.when(jnp.logical_and(c >= LAG, c < NC + LAG))
        def _():
            finish(0, c - LAG)
            apply_chunk(F2, O2, L2, 4, c - LAG)
            send_borders(1, c - LAG)

        @pl.when(c >= 2 * LAG)
        def _():
            finish(1, c - 2 * LAG)

    loop(NC + 2 * LAG, stage)

    three = U.at[:, pl.ds(0, 3 * OWN)]
    side = U.at[:, pl.ds(0, SIDE)]
    send(three, three, y_send.at[0], y_recv.at[0], partner).wait_send()
    send(side, side, z_send.at[0], z_recv.at[0], partner).wait_send()
    for n in range(2):
        XB = (XB1, XB2)[n].at[0, :, :, pl.ds(0, (MODES, SIDE)[n])]
        for up, present in ((1, has_high), (0, has_low)):
            pl.when(present)(send(XB, XB, x_send.at[n, up], x_recv.at[n, up, 0], partner).wait_send)
    for n in range(2):
        _, yy = borders(n)
        pl.when(y_high)(yy(True).wait_send)
        pl.when(y_low)(yy(False).wait_send)
    pl.when(has_high)(a_copy(True).wait_send)
    pl.when(has_low)(a_copy(False).wait_send)
    for n in range(2):
        pltpu.make_async_copy(own, own, o_loc.at[n]).wait()
        every = send(three, three, o_send.at[n], o_recv.at[n], partner)
        every.wait_send()
        every.wait_recv()


def per_device(field, coeff, pairs, values):
    vmem = pl.BlockSpec(memory_space=pltpu.VMEM)
    hbm = pl.BlockSpec(memory_space=pl.ANY)
    out = jax.ShapeDtypeStruct((OWN, LAYERS, 48, 1, 128), F32)
    sem = pltpu.SemaphoreType.DMA
    first, second = pl.pallas_call(
        kernel,
        out_shape=(out, out),
        in_specs=[hbm, hbm, vmem, vmem],
        out_specs=(vmem, vmem),
        scratch_shapes=[
            pltpu.VMEM((NC, MODES, LAYERS, NR, 1, 128), F32),
            pltpu.VMEM((NC, MODES, LAYERS, NR, 1, 128), F32),
            pltpu.VMEM((NC, 32, LAYERS, NR, 1, 128), F32),
            pltpu.VMEM((2, NC, NR, MODES, 128), F32),
            pltpu.VMEM((2, NC, NR, 32, 128), F32),
            pltpu.VMEM((2, LAYERS, MODES, 128), F32),
            pltpu.VMEM((2, LAYERS, 32, 128), F32),
            pltpu.VMEM((TERMS, 6, HIGH_ROWS, 1, 128), F32),
            pltpu.VMEM((CELLS * 36, 1, 128), F32),
            pltpu.VMEM((6, HIGH_ROWS, MODES, 128), F32),
            pltpu.VMEM((6, HIGH_ROWS, 32, 128), F32),
            pltpu.VMEM((336, 256), F32),
            pltpu.VMEM((336, 256), BF16),
            pltpu.VMEM((192, 256), BF16),
            sem((1,)),
            sem((NC,)),
            sem((1,)),
            sem((NC,)),
            sem((2,)),
            sem((2,)),
            sem((2, 2)),
            sem((2, 2, NC)),
            sem((2, 2)),
            sem((2, 2)),
            sem((2,)),
            sem((2,)),
            sem((4,)),
            sem((2,)),
        ],
        compiler_params=pltpu.CompilerParams(
            collective_id=0, has_side_effects=True, vmem_limit_bytes=60 << 20
        ),
    )(
        field.reshape(OWN, LAYERS, 48, 1, 128),
        coeff.reshape(TERMS, LAYERS, 48, 1, 128),
        jnp.transpose(pairs, (0, 2, 1)),
        values,
    )
    return first.reshape(field.shape), second.reshape(field.shape)


def solution(mesh):
    in_specs = (P("mode", "space", None, None), P(None, "space", None, None), P(), P())
    out_specs = (P("mode", "space", None, None), P("mode", "space", None, None))
    return jax.shard_map(
        per_device, mesh=mesh, in_specs=in_specs, out_specs=out_specs, check_vma=False
    )
```

```python
import functools

import jax
import jax.numpy as jnp
from jax import lax
from jax.experimental import pallas as pl
from jax.experimental.pallas import tpu as pltpu
from jax.sharding import PartitionSpec as P

MESH = pl.DeviceIdType.MESH
F32 = jnp.float32
BF16 = jnp.bfloat16

TERMS = 6
OWN = 7
SIDE = 28
MODES = 56
LAYERS = 4
ROWS = 12
CELLS = LAYERS * ROWS
FACES = 6
HIGH_ROWS = ROWS + 2
NR = 1
NC = ROWS // NR
AHEAD = 5
LAG = 4


def kernel(
    field,
    coeff,
    pairs,
    values,
    outs,
    U,
    F,
    S,
    XB1,
    XB2,
    YB1,
    YB2,
    A,
    FC,
    O1,
    O2,
    LF,
    L1,
    L2,
    y_send,
    y_recv,
    z_send,
    z_recv,
    c_send,
    c_recv,
    x_send,
    x_recv,
    b_send,
    b_recv,
    o_send,
    o_recv,
    loc,
    o_loc,
):
    first_out, second_out = outs.at[0], outs.at[1]
    space = lax.axis_index("space")
    mode = lax.axis_index("mode")
    y = mode // 2
    zhi = mode % 2

    def y_peer(step):
        return (space, lax.rem(y + step, 4) * 2 + zhi)

    partner = (space, y * 2 + 1 - zhi)

    def s_peer(step):
        return (space + step, mode)

    at_end = {1: space % 8 == 7, -1: space % 8 == 0}

    def near_peer(step):
        return (space + step, jnp.where(at_end[step], y * 2 + 1 - zhi, mode))

    def send(src, dst, ss, rs, dev):
        return pltpu.make_async_remote_copy(
            src_ref=src, dst_ref=dst, send_sem=ss, recv_sem=rs, device_id=dev, device_id_type=MESH
        )

    def loop(n, body):
        def step(i, carry):
            body(i)
            return carry

        lax.fori_loop(0, n, step, 0)

    has_low = space > 0
    has_high = space < 31
    y_low = y > 0
    y_high = y < 3

    def chunk_row(c):
        return NR * jnp.where(c % 2 == 0, c // 2, NC - 1 - c // 2)

    U2 = U.reshape(NC * MODES * LAYERS * NR, 128)
    F2 = F.reshape(NC * MODES * LAYERS * NR, 128)
    S2 = S.reshape(NC * 32 * LAYERS * NR, 128)
    A2 = A.reshape(TERMS * 6 * HIGH_ROWS, 128)
    FC2 = FC.reshape(CELLS * 36, 128)

    A2[...] = jnp.zeros(A2.shape, F32)

    barrier = pltpu.get_barrier_semaphore()
    for step in (1, 2, 3):
        pl.semaphore_signal(barrier, inc=1, device_id=y_peer(step), device_id_type=MESH)
    pl.semaphore_signal(barrier, inc=1, device_id=partner, device_id_type=MESH)

    expected = jnp.int32(4)
    for present, step in ((has_low, -1), (has_high, 1)):
        turned = jnp.logical_and(present, at_end[step])

        @pl.when(present)
        def _(step=step):
            pl.semaphore_signal(barrier, inc=1, device_id=s_peer(step), device_id_type=MESH)

        @pl.when(turned)
        def _(step=step):
            pl.semaphore_signal(barrier, inc=1, device_id=near_peer(step), device_id_type=MESH)

        expected = expected + present.astype(jnp.int32) + turned.astype(jnp.int32)
    pl.semaphore_wait(barrier, expected)

    def y_copy(step, c):
        to = lax.rem(y + step, 4)
        return send(
            field.at[:, :, pl.ds(to * ROWS + chunk_row(c), NR)],
            U.at[c, pl.ds(zhi * SIDE + y * OWN, OWN)],
            y_send.at[0],
            y_recv.at[c],
            y_peer(step),
        )

    def wait_y(c):
        three = U.at[c, pl.ds(0, 3 * OWN)]
        send(three, three, y_send.at[0], y_recv.at[c], partner).wait_recv()

    def own_rows(c):
        return field.at[:, :, pl.ds(y * ROWS + chunk_row(c), NR)]

    def z_copy(c, j):
        at = pl.ds(zhi * SIDE + lax.rem(y + j, 4) * OWN, OWN)
        src = own_rows(c) if j == 0 else U.at[c, at]
        return send(src, U.at[c, at], z_send.at[0], z_recv.at[c], partner)

    def wait_z(c):
        side = U.at[c, pl.ds((1 - zhi) * SIDE, SIDE)]
        send(side, side, z_send.at[0], z_recv.at[c], partner).wait_recv()

    def own_copy(c):
        return pltpu.make_async_copy(own_rows(c), U.at[c, pl.ds(zhi * SIDE + y * OWN, OWN)], loc.at[3])

    def start_field(c):
        for step in (1, 3, 2):
            y_copy(step, c).start()
        z_copy(c, 0).start()

    loop(NC, start_field)

    own_a = pltpu.make_async_copy(
        coeff.at[:, :, pl.ds(y * ROWS, ROWS)], A.at[:, pl.ds(1, LAYERS), pl.ds(1, ROWS)], loc.at[0]
    )
    low_a = pltpu.make_async_copy(
        coeff.at[:, :, pl.ds(jnp.maximum(y * ROWS - 1, 0), 1)],
        A.at[:, pl.ds(1, LAYERS), pl.ds(0, 1)],
        loc.at[1],
    )
    high_a = pltpu.make_async_copy(
        coeff.at[:, :, pl.ds(jnp.minimum(y * ROWS + ROWS, 47), 1)],
        A.at[:, pl.ds(1, LAYERS), pl.ds(ROWS + 1, 1)],
        loc.at[2],
    )

    def a_copy(up):
        l, slot, s = (LAYERS - 1, 0, 1) if up else (0, LAYERS + 1, -1)
        return send(
            coeff.at[:, l, pl.ds(y * ROWS, ROWS)],
            A.at[:, slot, pl.ds(1, ROWS)],
            c_send.at[int(up)],
            c_recv.at[int(up)],
            near_peer(s),
        )

    own_a.start()
    pl.when(y_low)(low_a.start)
    pl.when(y_high)(high_a.start)
    pl.when(has_high)(a_copy(True).start)
    pl.when(has_low)(a_copy(False).start)

    loop(NC, lambda c: own_copy(c).start())

    def y_to_z(c):
        wait_y(c)
        for j in (1, 2, 3):
            z_copy(c, j).start()

    loop(AHEAD, y_to_z)

    def mode_id(at):
        side = (at >= SIDE).astype(jnp.int32)
        rest = at - SIDE * side
        block = sum((rest >= OWN * n).astype(jnp.int32) for n in (1, 2, 3))
        return rest + OWN * block + OWN * side

    nnz = values.shape[1]
    eye = lax.broadcasted_iota(jnp.int32, (nnz, nnz), 0) == lax.broadcasted_iota(jnp.int32, (nnz, nnz), 1)
    slot = lax.broadcasted_iota(jnp.int32, (nnz, 256), 1) % 64
    col_id = jnp.where(slot < MODES, mode_id(slot), -1)
    low_part = lax.broadcasted_iota(jnp.int32, (8, 256), 1) >= 128

    def build(tiles, start, count, target):
        at = lax.broadcasted_iota(jnp.int32, (tiles * 8, nnz), 0)
        ids = jnp.where(at < count, mode_id(at + start), -1)

        def term(k):
            both = pairs[k]
            cols = jnp.sum(jnp.where(eye, both[1:2, :], 0), axis=1, keepdims=True)
            left = jnp.where(ids == both[0:1, :], values[pl.ds(k, 1), :], 0.0)
            right = jnp.where(col_id == cols, 1.0, 0.0)
            full = jnp.dot(left, right, precision=lax.Precision.HIGHEST, preferred_element_type=F32)
            for t in range(tiles):
                part = full[t * 8 : t * 8 + 8]
                high = part.astype(BF16).astype(F32)
                LF[pl.ds(pl.multiple_of(t * 48 + k * 8, 8), 8), :] = jnp.where(low_part, part - high, high)

        loop(TERMS, term)
        target[...] = LF[0 : tiles * 48, :].astype(BF16)

    build(7, 0, MODES, L1)
    build(4, zhi * SIDE, SIDE, L2)

    own_a.wait()
    pl.when(y_low)(low_a.wait)
    pl.when(y_high)(high_a.wait)
    pl.when(has_low)(a_copy(True).wait_recv)
    pl.when(has_high)(a_copy(False).wait_recv)
    lanes = lax.broadcasted_iota(jnp.int32, (ROWS, 128), 1)

    def faces(i):
        k = i // LAYERS
        l = lax.rem(i, LAYERS)
        base = (k * 6 + l + 1) * HIGH_ROWS + 1
        a = A2[pl.ds(base, ROWS), :]
        near = (
            A2[pl.ds(base - HIGH_ROWS, ROWS), :],
            A2[pl.ds(base + HIGH_ROWS, ROWS), :],
            A2[pl.ds(base - 1, ROWS), :],
            A2[pl.ds(base + 1, ROWS), :],
            jnp.where(lanes == 0, 0.0, pltpu.roll(a, 1, 1)),
            jnp.where(lanes == 127, 0.0, pltpu.roll(a, 127, 1)),
        )
        for d in range(FACES):
            FC2[pl.ds(l * (ROWS * 36) + d * 6 + k, ROWS, stride=36), :] = 0.5 * (a + near[d])

    loop(TERMS * LAYERS, faces)

    def clear(i):
        l = i // HIGH_ROWS
        r = lax.rem(i, HIGH_ROWS)
        O1[l, r] = jnp.zeros((MODES, 128), F32)
        O2[l, r] = jnp.zeros((32, 128), F32)

    loop(6 * HIGH_ROWS, clear)
    own = U.at[:, pl.ds(0, OWN)]
    pltpu.make_async_copy(own, own, loc.at[3]).wait()

    def mix(matrix, a, b):
        u = jnp.concatenate([a, b], axis=1)
        u = jnp.concatenate([u, jnp.zeros((8, 256), F32)], axis=0)
        high = u.astype(BF16)
        low = (u - high.astype(F32)).astype(BF16)
        return jnp.dot(
            matrix[...], jnp.concatenate([high, low, high, low], axis=0), preferred_element_type=F32
        )

    def face_sum(row, d, v):
        total = None
        for k in range(TERMS):
            term = FC2[pl.ds(row * 36 + d * 6 + k, 1), :] * v[k]
            total = term if total is None else total + term
        return total

    lane8 = lax.broadcasted_iota(jnp.int32, (8, 128), 1)

    def apply_chunk(src, O, matrix, tiles, c):
        def pair(p):
            i = p // 2
            l = 2 * lax.rem(p, 2)
            r = chunk_row(c) + i
            base = c * (MODES * LAYERS * NR) + l * NR + i
            full = mix(
                matrix,
                src[pl.ds(base, MODES, stride=LAYERS * NR), :],
                src[pl.ds(base + NR, MODES, stride=LAYERS * NR), :],
            )
            for h in range(2):
                at_l, at_r, row = l + 1 + h, r + 1, (l + h) * ROWS + r
                for t in range(tiles):
                    v = [full[t * 48 + k * 8 : t * 48 + k * 8 + 8, h * 128 : h * 128 + 128] for k in range(TERMS)]
                    xl, xr, yl, yr, zl, zr = [face_sum(row, d, v) for d in range(FACES)]
                    zl_moved = jnp.where(lane8 == 127, 0.0, pltpu.roll(zl, 127, 1))
                    zr_moved = jnp.where(lane8 == 0, 0.0, pltpu.roll(zr, 1, 1))
                    tile = pl.ds(t * 8, 8)
                    O[at_l, at_r, tile, :] += (xl + xr) + (yl + yr) + ((zl + zr) - (zl_moved + zr_moved))
                    O[at_l - 1, at_r, tile, :] -= xl
                    O[at_l + 1, at_r, tile, :] -= xr
                    O[at_l, at_r - 1, tile, :] -= yl
                    O[at_l, at_r + 1, tile, :] -= yr

        loop(2 * NR, pair)

    def borders(n):
        O, XB, YB, count = ((O1, XB1, YB1, MODES), (O2, XB2, YB2, SIDE))[n]
        some = pl.ds(0, count)

        def x(up, c):
            l, slot, s = (LAYERS + 1, 0, 1) if up else (0, 1, -1)
            return send(
                O.at[l, pl.ds(chunk_row(c) + 1, NR), some],
                XB.at[slot, c, :, some],
                x_send.at[n, int(up)],
                x_recv.at[n, int(up), c],
                (near_peer, s_peer)[n](s),
            )

        def yy(up):
            r, slot, s = (ROWS + 1, 0, 1) if up else (0, 1, 3)
            return send(
                O.at[pl.ds(1, LAYERS), r, some],
                YB.at[slot, :, some],
                b_send.at[n, int(up)],
                b_recv.at[n, int(up)],
                y_peer(s),
            )

        return x, yy

    def is_top(c):
        return c == 1

    def is_bottom(c):
        return c == 0

    def send_borders(n, c):
        x, yy = borders(n)
        pl.when(has_high)(x(True, c).start)
        pl.when(has_low)(x(False, c).start)
        pl.when(jnp.logical_and(y_high, is_top(c)))(yy(True).start)
        pl.when(jnp.logical_and(y_low, is_bottom(c)))(yy(False).start)

    def add_borders(n, c):
        x, yy = borders(n)
        O, XB, YB, modes = ((O1, XB1, YB1, MODES), (O2, XB2, YB2, 32))[n]
        r = chunk_row(c) + 1

        @pl.when(has_low)
        def _():
            x(True, c).wait_recv()
            for i in range(NR):
                O[1, r + i] += XB[0, c, i]

        @pl.when(has_high)
        def _():
            x(False, c).wait_recv()
            for i in range(NR):
                O[LAYERS, r + i] += XB[1, c, i]

        @pl.when(jnp.logical_and(y_low, is_bottom(c)))
        def _():
            yy(True).wait_recv()
            for l in range(LAYERS):
                O[l + 1, 1] += YB[0, l]

        @pl.when(jnp.logical_and(y_high, is_top(c)))
        def _():
            yy(False).wait_recv()
            for l in range(LAYERS):
                O[l + 1, ROWS] += YB[1, l]

    def out_copy(n, step, c):
        to = lax.rem(y + step, 4)
        if n == 0:
            src, dst = F.at[c, pl.ds(zhi * SIDE + to * OWN, OWN)], first_out
        else:
            src, dst = S.at[c, pl.ds(to * OWN, OWN)], second_out
        dst = dst.at[:, :, pl.ds(y * ROWS + chunk_row(c), NR)]
        if step == 0:
            return pltpu.make_async_copy(src, dst, o_loc.at[n])
        return send(src, dst, o_send.at[n], o_recv.at[n], y_peer(step))

    def finish(n, c):
        add_borders(n, c)
        O, to, modes = ((O1, F2, MODES), (O2, S2, 32))[n]
        r = chunk_row(c) + 1
        for i in range(NR):
            for l in range(LAYERS):
                to[pl.ds(c * (modes * LAYERS * NR) + l * NR + i, modes, stride=LAYERS * NR), :] = O[l + 1, r + i]
        for step in (2, 1, 3, 0):
            out_copy(n, step, c).start()

    def stage(c):
        @pl.when(c < NC)
        def _():
            wait_z(c)
            apply_chunk(U2, O1, L1, 7, c)
            send_borders(0, c)

        @pl.when(c + AHEAD < NC)
        def _():
            y_to_z(c + AHEAD)

        @pl.when(jnp.logical_and(c >= LAG, c < NC + LAG))
        def _():
            finish(0, c - LAG)
            apply_chunk(F2, O2, L2, 4, c - LAG)
            send_borders(1, c - LAG)

        @pl.when(c >= 2 * LAG)
        def _():
            finish(1, c - 2 * LAG)

    loop(NC + 2 * LAG, stage)

    three = U.at[:, pl.ds(0, 3 * OWN)]
    side = U.at[:, pl.ds(0, SIDE)]
    send(three, three, y_send.at[0], y_recv.at[0], partner).wait_send()
    send(side, side, z_send.at[0], z_recv.at[0], partner).wait_send()
    for n in range(2):
        XB = (XB1, XB2)[n].at[0, :, :, pl.ds(0, (MODES, SIDE)[n])]
        for up, present in ((1, has_high), (0, has_low)):
            pl.when(present)(send(XB, XB, x_send.at[n, up], x_recv.at[n, up, 0], partner).wait_send)
    for n in range(2):
        _, yy = borders(n)
        pl.when(y_high)(yy(True).wait_send)
        pl.when(y_low)(yy(False).wait_send)
    pl.when(has_high)(a_copy(True).wait_send)
    pl.when(has_low)(a_copy(False).wait_send)
    for n in range(2):
        pltpu.make_async_copy(own, own, o_loc.at[n]).wait()
        every = send(three, three, o_send.at[n], o_recv.at[n], partner)
        every.wait_send()
        every.wait_recv()


def per_device(field, coeff, pairs, values):
    vmem = pl.BlockSpec(memory_space=pltpu.VMEM)
    hbm = pl.BlockSpec(memory_space=pl.ANY)
    out = jax.ShapeDtypeStruct((2, OWN, LAYERS, 48, 1, 128), F32)
    sem = pltpu.SemaphoreType.DMA
    both = pl.pallas_call(
        kernel,
        out_shape=out,
        in_specs=[hbm, hbm, vmem, vmem],
        out_specs=hbm,
        scratch_shapes=[
            pltpu.VMEM((NC, MODES, LAYERS, NR, 1, 128), F32),
            pltpu.VMEM((NC, MODES, LAYERS, NR, 1, 128), F32),
            pltpu.VMEM((NC, 32, LAYERS, NR, 1, 128), F32),
            pltpu.VMEM((2, NC, NR, MODES, 128), F32),
            pltpu.VMEM((2, NC, NR, 32, 128), F32),
            pltpu.VMEM((2, LAYERS, MODES, 128), F32),
            pltpu.VMEM((2, LAYERS, 32, 128), F32),
            pltpu.VMEM((TERMS, 6, HIGH_ROWS, 1, 128), F32),
            pltpu.VMEM((CELLS * 36, 1, 128), F32),
            pltpu.VMEM((6, HIGH_ROWS, MODES, 128), F32),
            pltpu.VMEM((6, HIGH_ROWS, 32, 128), F32),
            pltpu.VMEM((336, 256), F32),
            pltpu.VMEM((336, 256), BF16),
            pltpu.VMEM((192, 256), BF16),
            sem((1,)),
            sem((NC,)),
            sem((1,)),
            sem((NC,)),
            sem((2,)),
            sem((2,)),
            sem((2, 2)),
            sem((2, 2, NC)),
            sem((2, 2)),
            sem((2, 2)),
            sem((2,)),
            sem((2,)),
            sem((4,)),
            sem((2,)),
        ],
        compiler_params=pltpu.CompilerParams(
            collective_id=0, has_side_effects=True, vmem_limit_bytes=60 << 20
        ),
    )(
        field.reshape(OWN, LAYERS, 48, 1, 128),
        coeff.reshape(TERMS, LAYERS, 48, 1, 128),
        jnp.transpose(pairs, (0, 2, 1)),
        values,
    )
    return both[0].reshape(field.shape), both[1].reshape(field.shape)


def solution(mesh):
    in_specs = (P("mode", "space", None, None), P(None, "space", None, None), P(), P())
    out_specs = (P("mode", "space", None, None), P("mode", "space", None, None))
    return jax.shard_map(
        per_device, mesh=mesh, in_specs=in_specs, out_specs=out_specs, check_vma=False
    )
```

```python
import functools

import jax
import jax.numpy as jnp
from jax import lax
from jax.experimental import pallas as pl
from jax.experimental.pallas import tpu as pltpu
from jax.sharding import PartitionSpec as P

MESH = pl.DeviceIdType.MESH
F32 = jnp.float32
BF16 = jnp.bfloat16

TERMS = 6
OWN = 7
SIDE = 28
MODES = 56
LAYERS = 4
ROWS = 12
CELLS = LAYERS * ROWS
FACES = 6
HIGH_ROWS = ROWS + 2
NR = 1
NC = ROWS // NR
AHEAD = 5
AT_ONCE = 8
LAG = 4


def kernel(
    field,
    coeff,
    pairs,
    values,
    outs,
    U,
    F,
    S,
    XB1,
    XB2,
    YB1,
    YB2,
    A,
    FC,
    O1,
    O2,
    LF,
    L1,
    L2,
    y_send,
    y_recv,
    z_send,
    z_recv,
    c_send,
    c_recv,
    x_send,
    x_recv,
    b_send,
    b_recv,
    o_send,
    o_recv,
    loc,
    o_loc,
):
    first_out, second_out = outs.at[0], outs.at[1]
    space = lax.axis_index("space")
    mode = lax.axis_index("mode")
    y = mode // 2
    zhi = mode % 2

    def y_peer(step):
        return (space, lax.rem(y + step, 4) * 2 + zhi)

    partner = (space, y * 2 + 1 - zhi)

    def s_peer(step):
        return (space + step, mode)

    at_end = {1: space % 8 == 7, -1: space % 8 == 0}

    def near_peer(step):
        return (space + step, jnp.where(at_end[step], y * 2 + 1 - zhi, mode))

    def send(src, dst, ss, rs, dev):
        return pltpu.make_async_remote_copy(
            src_ref=src, dst_ref=dst, send_sem=ss, recv_sem=rs, device_id=dev, device_id_type=MESH
        )

    def loop(n, body):
        def step(i, carry):
            body(i)
            return carry

        lax.fori_loop(0, n, step, 0)

    has_low = space > 0
    has_high = space < 31
    y_low = y > 0
    y_high = y < 3

    def chunk_row(c):
        return NR * jnp.where(c % 2 == 0, c // 2, NC - 1 - c // 2)

    U2 = U.reshape(NC * MODES * LAYERS * NR, 128)
    F2 = F.reshape(NC * MODES * LAYERS * NR, 128)
    S2 = S.reshape(NC * 32 * LAYERS * NR, 128)
    A2 = A.reshape(TERMS * 6 * HIGH_ROWS, 128)
    FC2 = FC.reshape(CELLS * 36, 128)

    A2[...] = jnp.zeros(A2.shape, F32)

    barrier = pltpu.get_barrier_semaphore()
    for step in (1, 2, 3):
        pl.semaphore_signal(barrier, inc=1, device_id=y_peer(step), device_id_type=MESH)
    pl.semaphore_signal(barrier, inc=1, device_id=partner, device_id_type=MESH)

    expected = jnp.int32(4)
    for present, step in ((has_low, -1), (has_high, 1)):
        turned = jnp.logical_and(present, at_end[step])

        @pl.when(present)
        def _(step=step):
            pl.semaphore_signal(barrier, inc=1, device_id=s_peer(step), device_id_type=MESH)

        @pl.when(turned)
        def _(step=step):
            pl.semaphore_signal(barrier, inc=1, device_id=near_peer(step), device_id_type=MESH)

        expected = expected + present.astype(jnp.int32) + turned.astype(jnp.int32)
    pl.semaphore_wait(barrier, expected)

    def y_copy(step, c):
        to = lax.rem(y + step, 4)
        return send(
            field.at[:, :, pl.ds(to * ROWS + chunk_row(c), NR)],
            U.at[c, pl.ds(zhi * SIDE + y * OWN, OWN)],
            y_send.at[0],
            y_recv.at[c],
            y_peer(step),
        )

    def wait_y(c):
        three = U.at[c, pl.ds(0, 3 * OWN)]
        send(three, three, y_send.at[0], y_recv.at[c], partner).wait_recv()

    def own_rows(c):
        return field.at[:, :, pl.ds(y * ROWS + chunk_row(c), NR)]

    def z_copy(c, j):
        at = pl.ds(zhi * SIDE + lax.rem(y + j, 4) * OWN, OWN)
        src = own_rows(c) if j == 0 else U.at[c, at]
        return send(src, U.at[c, at], z_send.at[0], z_recv.at[c], partner)

    def wait_z(c):
        side = U.at[c, pl.ds((1 - zhi) * SIDE, SIDE)]
        send(side, side, z_send.at[0], z_recv.at[c], partner).wait_recv()

    def own_copy(c):
        return pltpu.make_async_copy(own_rows(c), U.at[c, pl.ds(zhi * SIDE + y * OWN, OWN)], loc.at[3])

    def start_field(c):
        for step in (1, 3, 2):
            y_copy(step, c).start()

        @pl.when(c < AT_ONCE)
        def _():
            z_copy(c, 0).start()

    loop(NC, start_field)

    own_a = pltpu.make_async_copy(
        coeff.at[:, :, pl.ds(y * ROWS, ROWS)], A.at[:, pl.ds(1, LAYERS), pl.ds(1, ROWS)], loc.at[0]
    )
    low_a = pltpu.make_async_copy(
        coeff.at[:, :, pl.ds(jnp.maximum(y * ROWS - 1, 0), 1)],
        A.at[:, pl.ds(1, LAYERS), pl.ds(0, 1)],
        loc.at[1],
    )
    high_a = pltpu.make_async_copy(
        coeff.at[:, :, pl.ds(jnp.minimum(y * ROWS + ROWS, 47), 1)],
        A.at[:, pl.ds(1, LAYERS), pl.ds(ROWS + 1, 1)],
        loc.at[2],
    )

    def a_copy(up):
        l, slot, s = (LAYERS - 1, 0, 1) if up else (0, LAYERS + 1, -1)
        return send(
            coeff.at[:, l, pl.ds(y * ROWS, ROWS)],
            A.at[:, slot, pl.ds(1, ROWS)],
            c_send.at[int(up)],
            c_recv.at[int(up)],
            near_peer(s),
        )

    own_a.start()
    pl.when(y_low)(low_a.start)
    pl.when(y_high)(high_a.start)
    pl.when(has_high)(a_copy(True).start)
    pl.when(has_low)(a_copy(False).start)

    loop(NC, lambda c: own_copy(c).start())

    def y_to_z(c):
        @pl.when(c >= AT_ONCE)
        def _():
            z_copy(c, 0).start()

        wait_y(c)
        for j in (1, 2, 3):
            z_copy(c, j).start()

    loop(AHEAD, y_to_z)

    def mode_id(at):
        side = (at >= SIDE).astype(jnp.int32)
        rest = at - SIDE * side
        block = sum((rest >= OWN * n).astype(jnp.int32) for n in (1, 2, 3))
        return rest + OWN * block + OWN * side

    nnz = values.shape[1]
    eye = lax.broadcasted_iota(jnp.int32, (nnz, nnz), 0) == lax.broadcasted_iota(jnp.int32, (nnz, nnz), 1)
    slot = lax.broadcasted_iota(jnp.int32, (nnz, 256), 1) % 64
    col_id = jnp.where(slot < MODES, mode_id(slot), -1)
    low_part = lax.broadcasted_iota(jnp.int32, (8, 256), 1) >= 128

    def build(tiles, start, count, target):
        at = lax.broadcasted_iota(jnp.int32, (tiles * 8, nnz), 0)
        ids = jnp.where(at < count, mode_id(at + start), -1)

        def term(k):
            both = pairs[k]
            cols = jnp.sum(jnp.where(eye, both[1:2, :], 0), axis=1, keepdims=True)
            left = jnp.where(ids == both[0:1, :], values[pl.ds(k, 1), :], 0.0)
            right = jnp.where(col_id == cols, 1.0, 0.0)
            full = jnp.dot(left, right, precision=lax.Precision.HIGHEST, preferred_element_type=F32)
            for t in range(tiles):
                part = full[t * 8 : t * 8 + 8]
                high = part.astype(BF16).astype(F32)
                LF[pl.ds(pl.multiple_of(t * 48 + k * 8, 8), 8), :] = jnp.where(low_part, part - high, high)

        loop(TERMS, term)
        target[...] = LF[0 : tiles * 48, :].astype(BF16)

    build(7, 0, MODES, L1)
    build(4, zhi * SIDE, SIDE, L2)

    own_a.wait()
    pl.when(y_low)(low_a.wait)
    pl.when(y_high)(high_a.wait)
    pl.when(has_low)(a_copy(True).wait_recv)
    pl.when(has_high)(a_copy(False).wait_recv)
    lanes = lax.broadcasted_iota(jnp.int32, (ROWS, 128), 1)

    def faces(i):
        k = i // LAYERS
        l = lax.rem(i, LAYERS)
        base = (k * 6 + l + 1) * HIGH_ROWS + 1
        a = A2[pl.ds(base, ROWS), :]
        near = (
            A2[pl.ds(base - HIGH_ROWS, ROWS), :],
            A2[pl.ds(base + HIGH_ROWS, ROWS), :],
            A2[pl.ds(base - 1, ROWS), :],
            A2[pl.ds(base + 1, ROWS), :],
            jnp.where(lanes == 0, 0.0, pltpu.roll(a, 1, 1)),
            jnp.where(lanes == 127, 0.0, pltpu.roll(a, 127, 1)),
        )
        for d in range(FACES):
            FC2[pl.ds(l * (ROWS * 36) + d * 6 + k, ROWS, stride=36), :] = 0.5 * (a + near[d])

    loop(TERMS * LAYERS, faces)

    def clear(i):
        l = i // HIGH_ROWS
        r = lax.rem(i, HIGH_ROWS)
        O1[l, r] = jnp.zeros((MODES, 128), F32)
        O2[l, r] = jnp.zeros((32, 128), F32)

    loop(6 * HIGH_ROWS, clear)
    own = U.at[:, pl.ds(0, OWN)]
    pltpu.make_async_copy(own, own, loc.at[3]).wait()

    def mix(matrix, a, b):
        u = jnp.concatenate([a, b], axis=1)
        u = jnp.concatenate([u, jnp.zeros((8, 256), F32)], axis=0)
        high = u.astype(BF16)
        low = (u - high.astype(F32)).astype(BF16)
        return jnp.dot(
            matrix[...], jnp.concatenate([high, low, high, low], axis=0), preferred_element_type=F32
        )

    def face_sum(row, d, v):
        total = None
        for k in range(TERMS):
            term = FC2[pl.ds(row * 36 + d * 6 + k, 1), :] * v[k]
            total = term if total is None else total + term
        return total

    lane8 = lax.broadcasted_iota(jnp.int32, (8, 128), 1)

    def apply_chunk(src, O, matrix, tiles, c):
        def pair(p):
            i = p // 2
            l = 2 * lax.rem(p, 2)
            r = chunk_row(c) + i
            base = c * (MODES * LAYERS * NR) + l * NR + i
            full = mix(
                matrix,
                src[pl.ds(base, MODES, stride=LAYERS * NR), :],
                src[pl.ds(base + NR, MODES, stride=LAYERS * NR), :],
            )
            for h in range(2):
                at_l, at_r, row = l + 1 + h, r + 1, (l + h) * ROWS + r
                for t in range(tiles):
                    v = [full[t * 48 + k * 8 : t * 48 + k * 8 + 8, h * 128 : h * 128 + 128] for k in range(TERMS)]
                    xl, xr, yl, yr, zl, zr = [face_sum(row, d, v) for d in range(FACES)]
                    zl_moved = jnp.where(lane8 == 127, 0.0, pltpu.roll(zl, 127, 1))
                    zr_moved = jnp.where(lane8 == 0, 0.0, pltpu.roll(zr, 1, 1))
                    tile = pl.ds(t * 8, 8)
                    O[at_l, at_r, tile, :] += (xl + xr) + (yl + yr) + ((zl + zr) - (zl_moved + zr_moved))
                    O[at_l - 1, at_r, tile, :] -= xl
                    O[at_l + 1, at_r, tile, :] -= xr
                    O[at_l, at_r - 1, tile, :] -= yl
                    O[at_l, at_r + 1, tile, :] -= yr

        loop(2 * NR, pair)

    def borders(n):
        O, XB, YB, count = ((O1, XB1, YB1, MODES), (O2, XB2, YB2, SIDE))[n]
        some = pl.ds(0, count)

        def x(up, c):
            l, slot, s = (LAYERS + 1, 0, 1) if up else (0, 1, -1)
            return send(
                O.at[l, pl.ds(chunk_row(c) + 1, NR), some],
                XB.at[slot, c, :, some],
                x_send.at[n, int(up)],
                x_recv.at[n, int(up), c],
                (near_peer, s_peer)[n](s),
            )

        def yy(up):
            r, slot, s = (ROWS + 1, 0, 1) if up else (0, 1, 3)
            return send(
                O.at[pl.ds(1, LAYERS), r, some],
                YB.at[slot, :, some],
                b_send.at[n, int(up)],
                b_recv.at[n, int(up)],
                y_peer(s),
            )

        return x, yy

    def is_top(c):
        return c == 1

    def is_bottom(c):
        return c == 0

    def send_borders(n, c):
        x, yy = borders(n)
        pl.when(has_high)(x(True, c).start)
        pl.when(has_low)(x(False, c).start)
        pl.when(jnp.logical_and(y_high, is_top(c)))(yy(True).start)
        pl.when(jnp.logical_and(y_low, is_bottom(c)))(yy(False).start)

    def add_borders(n, c):
        x, yy = borders(n)
        O, XB, YB, modes = ((O1, XB1, YB1, MODES), (O2, XB2, YB2, 32))[n]
        r = chunk_row(c) + 1

        @pl.when(has_low)
        def _():
            x(True, c).wait_recv()
            for i in range(NR):
                O[1, r + i] += XB[0, c, i]

        @pl.when(has_high)
        def _():
            x(False, c).wait_recv()
            for i in range(NR):
                O[LAYERS, r + i] += XB[1, c, i]

        @pl.when(jnp.logical_and(y_low, is_bottom(c)))
        def _():
            yy(True).wait_recv()
            for l in range(LAYERS):
                O[l + 1, 1] += YB[0, l]

        @pl.when(jnp.logical_and(y_high, is_top(c)))
        def _():
            yy(False).wait_recv()
            for l in range(LAYERS):
                O[l + 1, ROWS] += YB[1, l]

    def out_copy(n, step, c):
        to = lax.rem(y + step, 4)
        if n == 0:
            src, dst = F.at[c, pl.ds(zhi * SIDE + to * OWN, OWN)], first_out
        else:
            src, dst = S.at[c, pl.ds(to * OWN, OWN)], second_out
        dst = dst.at[:, :, pl.ds(y * ROWS + chunk_row(c), NR)]
        if step == 0:
            return pltpu.make_async_copy(src, dst, o_loc.at[n])
        return send(src, dst, o_send.at[n], o_recv.at[n], y_peer(step))

    def finish(n, c):
        add_borders(n, c)
        O, to, modes = ((O1, F2, MODES), (O2, S2, 32))[n]
        r = chunk_row(c) + 1
        for i in range(NR):
            for l in range(LAYERS):
                to[pl.ds(c * (modes * LAYERS * NR) + l * NR + i, modes, stride=LAYERS * NR), :] = O[l + 1, r + i]
        for step in (2, 1, 3, 0):
            out_copy(n, step, c).start()

    def stage(c):
        @pl.when(c < NC)
        def _():
            wait_z(c)
            apply_chunk(U2, O1, L1, 7, c)
            send_borders(0, c)

        @pl.when(c + AHEAD < NC)
        def _():
            y_to_z(c + AHEAD)

        @pl.when(jnp.logical_and(c >= LAG, c < NC + LAG))
        def _():
            finish(0, c - LAG)
            apply_chunk(F2, O2, L2, 4, c - LAG)
            send_borders(1, c - LAG)

        @pl.when(c >= 2 * LAG)
        def _():
            finish(1, c - 2 * LAG)

    loop(NC + 2 * LAG, stage)

    three = U.at[:, pl.ds(0, 3 * OWN)]
    side = U.at[:, pl.ds(0, SIDE)]
    send(three, three, y_send.at[0], y_recv.at[0], partner).wait_send()
    send(side, side, z_send.at[0], z_recv.at[0], partner).wait_send()
    for n in range(2):
        XB = (XB1, XB2)[n].at[0, :, :, pl.ds(0, (MODES, SIDE)[n])]
        for up, present in ((1, has_high), (0, has_low)):
            pl.when(present)(send(XB, XB, x_send.at[n, up], x_recv.at[n, up, 0], partner).wait_send)
    for n in range(2):
        _, yy = borders(n)
        pl.when(y_high)(yy(True).wait_send)
        pl.when(y_low)(yy(False).wait_send)
    pl.when(has_high)(a_copy(True).wait_send)
    pl.when(has_low)(a_copy(False).wait_send)
    for n in range(2):
        pltpu.make_async_copy(own, own, o_loc.at[n]).wait()
        every = send(three, three, o_send.at[n], o_recv.at[n], partner)
        every.wait_send()
        every.wait_recv()


def per_device(field, coeff, pairs, values):
    vmem = pl.BlockSpec(memory_space=pltpu.VMEM)
    hbm = pl.BlockSpec(memory_space=pl.ANY)
    out = jax.ShapeDtypeStruct((2, OWN, LAYERS, 48, 1, 128), F32)
    sem = pltpu.SemaphoreType.DMA
    both = pl.pallas_call(
        kernel,
        out_shape=out,
        in_specs=[hbm, hbm, vmem, vmem],
        out_specs=hbm,
        scratch_shapes=[
            pltpu.VMEM((NC, MODES, LAYERS, NR, 1, 128), F32),
            pltpu.VMEM((NC, MODES, LAYERS, NR, 1, 128), F32),
            pltpu.VMEM((NC, 32, LAYERS, NR, 1, 128), F32),
            pltpu.VMEM((2, NC, NR, MODES, 128), F32),
            pltpu.VMEM((2, NC, NR, 32, 128), F32),
            pltpu.VMEM((2, LAYERS, MODES, 128), F32),
            pltpu.VMEM((2, LAYERS, 32, 128), F32),
            pltpu.VMEM((TERMS, 6, HIGH_ROWS, 1, 128), F32),
            pltpu.VMEM((CELLS * 36, 1, 128), F32),
            pltpu.VMEM((6, HIGH_ROWS, MODES, 128), F32),
            pltpu.VMEM((6, HIGH_ROWS, 32, 128), F32),
            pltpu.VMEM((336, 256), F32),
            pltpu.VMEM((336, 256), BF16),
            pltpu.VMEM((192, 256), BF16),
            sem((1,)),
            sem((NC,)),
            sem((1,)),
            sem((NC,)),
            sem((2,)),
            sem((2,)),
            sem((2, 2)),
            sem((2, 2, NC)),
            sem((2, 2)),
            sem((2, 2)),
            sem((2,)),
            sem((2,)),
            sem((4,)),
            sem((2,)),
        ],
        compiler_params=pltpu.CompilerParams(
            collective_id=0, has_side_effects=True, vmem_limit_bytes=60 << 20
        ),
    )(
        field.reshape(OWN, LAYERS, 48, 1, 128),
        coeff.reshape(TERMS, LAYERS, 48, 1, 128),
        jnp.transpose(pairs, (0, 2, 1)),
        values,
    )
    def place(x, a, b):
        a[...] = x[0]
        b[...] = x[1]

    rows = OWN * LAYERS * 48
    flat = jax.ShapeDtypeStruct((rows, 128), F32)
    block = pl.BlockSpec((rows // 2, 128), lambda i: (i, 0))
    first, second = pl.pallas_call(
        place,
        grid=(2,),
        out_shape=(flat, flat),
        in_specs=[pl.BlockSpec((2, rows // 2, 128), lambda i: (0, i, 0))],
        out_specs=(block, block),
    )(both.reshape(2, rows, 128))
    return first.reshape(field.shape), second.reshape(field.shape)


def solution(mesh):
    in_specs = (P("mode", "space", None, None), P(None, "space", None, None), P(), P())
    out_specs = (P("mode", "space", None, None), P("mode", "space", None, None))
    return jax.shard_map(
        per_device, mesh=mesh, in_specs=in_specs, out_specs=out_specs, check_vma=False
    )
```

```python
import functools

import jax
import jax.numpy as jnp
from jax import lax
from jax.experimental import pallas as pl
from jax.experimental.pallas import tpu as pltpu
from jax.sharding import PartitionSpec as P

MESH = pl.DeviceIdType.MESH
F32 = jnp.float32
BF16 = jnp.bfloat16

TERMS = 6
OWN = 7
SIDE = 28
MODES = 56
LAYERS = 4
ROWS = 12
CELLS = LAYERS * ROWS
FACES = 6
HIGH_ROWS = ROWS + 2
NR = 1
NC = ROWS // NR
AHEAD = 5
AT_ONCE = 8
LAG = 4


def kernel(
    field,
    coeff,
    pairs,
    values,
    outs,
    U,
    F,
    S,
    XB1,
    XB2,
    YB1,
    YB2,
    A,
    FC,
    O1,
    O2,
    LF,
    L1,
    L2,
    y_send,
    y_recv,
    z_send,
    z_recv,
    c_send,
    c_recv,
    x_send,
    x_recv,
    b_send,
    b_recv,
    o_send,
    o_recv,
    loc,
    o_loc,
):
    first_out, second_out = outs.at[0], outs.at[1]
    space = lax.axis_index("space")
    mode = lax.axis_index("mode")
    y = mode // 2
    zhi = mode % 2

    def y_peer(step):
        return (space, lax.rem(y + step, 4) * 2 + zhi)

    partner = (space, y * 2 + 1 - zhi)

    def s_peer(step):
        return (space + step, mode)

    at_end = {1: space % 8 == 7, -1: space % 8 == 0}

    def near_peer(step):
        return (space + step, jnp.where(at_end[step], y * 2 + 1 - zhi, mode))

    def send(src, dst, ss, rs, dev):
        return pltpu.make_async_remote_copy(
            src_ref=src, dst_ref=dst, send_sem=ss, recv_sem=rs, device_id=dev, device_id_type=MESH
        )

    def loop(n, body):
        def step(i, carry):
            body(i)
            return carry

        lax.fori_loop(0, n, step, 0)

    has_low = space > 0
    has_high = space < 31
    y_low = y > 0
    y_high = y < 3

    def chunk_row(c):
        return NR * jnp.where(c % 2 == 0, c // 2, NC - 1 - c // 2)

    U2 = U.reshape(NC * MODES * LAYERS * NR, 128)
    F2 = F.reshape(NC * MODES * LAYERS * NR, 128)
    S2 = S.reshape(NC * 32 * LAYERS * NR, 128)
    A2 = A.reshape((TERMS + 1) * 6 * HIGH_ROWS, 128)
    FC2 = FC.reshape((CELLS + 8) * 36, 128)

    A2[...] = jnp.zeros(A2.shape, F32)

    barrier = pltpu.get_barrier_semaphore()
    for step in (1, 2, 3):
        pl.semaphore_signal(barrier, inc=1, device_id=y_peer(step), device_id_type=MESH)
    pl.semaphore_signal(barrier, inc=1, device_id=partner, device_id_type=MESH)

    expected = jnp.int32(4)
    for present, step in ((has_low, -1), (has_high, 1)):
        turned = jnp.logical_and(present, at_end[step])

        @pl.when(present)
        def _(step=step):
            pl.semaphore_signal(barrier, inc=1, device_id=s_peer(step), device_id_type=MESH)

        @pl.when(turned)
        def _(step=step):
            pl.semaphore_signal(barrier, inc=1, device_id=near_peer(step), device_id_type=MESH)

        expected = expected + present.astype(jnp.int32) + turned.astype(jnp.int32)
    pl.semaphore_wait(barrier, expected)

    def y_copy(step, c):
        to = lax.rem(y + step, 4)
        return send(
            field.at[:, :, pl.ds(to * ROWS + chunk_row(c), NR)],
            U.at[c, pl.ds(zhi * SIDE + y * OWN, OWN)],
            y_send.at[0],
            y_recv.at[c],
            y_peer(step),
        )

    def wait_y(c):
        three = U.at[c, pl.ds(0, 3 * OWN)]
        send(three, three, y_send.at[0], y_recv.at[c], partner).wait_recv()

    def own_rows(c):
        return field.at[:, :, pl.ds(y * ROWS + chunk_row(c), NR)]

    def z_copy(c, j):
        at = pl.ds(zhi * SIDE + lax.rem(y + j, 4) * OWN, OWN)
        src = own_rows(c) if j == 0 else U.at[c, at]
        return send(src, U.at[c, at], z_send.at[0], z_recv.at[c], partner)

    def wait_z(c):
        side = U.at[c, pl.ds((1 - zhi) * SIDE, SIDE)]
        send(side, side, z_send.at[0], z_recv.at[c], partner).wait_recv()

    def own_copy(c):
        return pltpu.make_async_copy(own_rows(c), U.at[c, pl.ds(zhi * SIDE + y * OWN, OWN)], loc.at[3])

    def start_field(c):
        for step in (1, 3, 2):
            y_copy(step, c).start()

        @pl.when(c < AT_ONCE)
        def _():
            z_copy(c, 0).start()

    loop(NC, start_field)

    own_a = pltpu.make_async_copy(
        coeff.at[:, :, pl.ds(y * ROWS, ROWS)], A.at[pl.ds(0, TERMS), pl.ds(1, LAYERS), pl.ds(1, ROWS)], loc.at[0]
    )
    low_a = pltpu.make_async_copy(
        coeff.at[:, :, pl.ds(jnp.maximum(y * ROWS - 1, 0), 1)],
        A.at[pl.ds(0, TERMS), pl.ds(1, LAYERS), pl.ds(0, 1)],
        loc.at[1],
    )
    high_a = pltpu.make_async_copy(
        coeff.at[:, :, pl.ds(jnp.minimum(y * ROWS + ROWS, 47), 1)],
        A.at[pl.ds(0, TERMS), pl.ds(1, LAYERS), pl.ds(ROWS + 1, 1)],
        loc.at[2],
    )

    def a_copy(up):
        l, slot, s = (LAYERS - 1, 0, 1) if up else (0, LAYERS + 1, -1)
        return send(
            coeff.at[:, l, pl.ds(y * ROWS, ROWS)],
            A.at[pl.ds(0, TERMS), slot, pl.ds(1, ROWS)],
            c_send.at[int(up)],
            c_recv.at[int(up)],
            near_peer(s),
        )

    own_a.start()
    pl.when(y_low)(low_a.start)
    pl.when(y_high)(high_a.start)
    pl.when(has_high)(a_copy(True).start)
    pl.when(has_low)(a_copy(False).start)

    loop(NC, lambda c: own_copy(c).start())

    def y_to_z(c):
        @pl.when(c >= AT_ONCE)
        def _():
            z_copy(c, 0).start()

        wait_y(c)
        for j in (1, 2, 3):
            z_copy(c, j).start()

    loop(AHEAD, y_to_z)

    def mode_id(at):
        side = (at >= SIDE).astype(jnp.int32)
        rest = at - SIDE * side
        block = sum((rest >= OWN * n).astype(jnp.int32) for n in (1, 2, 3))
        return rest + OWN * block + OWN * side

    nnz = values.shape[1]
    eye = lax.broadcasted_iota(jnp.int32, (nnz, nnz), 0) == lax.broadcasted_iota(jnp.int32, (nnz, nnz), 1)
    slot = lax.broadcasted_iota(jnp.int32, (nnz, 256), 1) % 64
    col_id = jnp.where(slot < MODES, mode_id(slot), -1)
    low_part = lax.broadcasted_iota(jnp.int32, (8, 256), 1) >= 128

    def build(tiles, start, count, target):
        at = lax.broadcasted_iota(jnp.int32, (tiles * 8, nnz), 0)
        ids = jnp.where(at < count, mode_id(at + start), -1)

        def term(k):
            both = pairs[k]
            cols = jnp.sum(jnp.where(eye, both[1:2, :], 0), axis=1, keepdims=True)
            left = jnp.where(ids == both[0:1, :], values[pl.ds(k, 1), :], 0.0)
            right = jnp.where(col_id == cols, 1.0, 0.0)
            full = jnp.dot(left, right, precision=lax.Precision.HIGHEST, preferred_element_type=F32)
            for t in range(tiles):
                part = full[t * 8 : t * 8 + 8]
                high = part.astype(BF16).astype(F32)
                LF[pl.ds(pl.multiple_of(t * 48 + k * 8, 8), 8), :] = jnp.where(low_part, part - high, high)

        loop(TERMS, term)
        target[...] = LF[0 : tiles * 48, :].astype(BF16)

    build(7, 0, MODES, L1)
    build(4, zhi * SIDE, SIDE, L2)

    own_a.wait()
    pl.when(y_low)(low_a.wait)
    pl.when(y_high)(high_a.wait)
    pl.when(has_low)(a_copy(True).wait_recv)
    pl.when(has_high)(a_copy(False).wait_recv)
    lanes = lax.broadcasted_iota(jnp.int32, (ROWS, 128), 1)

    def faces(i):
        k = i // LAYERS
        l = lax.rem(i, LAYERS)
        base = (k * 6 + l + 1) * HIGH_ROWS + 1
        a = A2[pl.ds(base, ROWS), :]
        near = (
            A2[pl.ds(base - HIGH_ROWS, ROWS), :],
            A2[pl.ds(base + HIGH_ROWS, ROWS), :],
            A2[pl.ds(base - 1, ROWS), :],
            A2[pl.ds(base + 1, ROWS), :],
            jnp.where(lanes == 0, 0.0, pltpu.roll(a, 1, 1)),
            jnp.where(lanes == 127, 0.0, pltpu.roll(a, 127, 1)),
        )
        for d in range(FACES):
            FC2[pl.ds(l * (ROWS * 36) + d * 6 + k, ROWS, stride=36), :] = 0.5 * (a + near[d])

    loop(TERMS * LAYERS, faces)

    def clear(i):
        l = i // HIGH_ROWS
        r = lax.rem(i, HIGH_ROWS)
        O1[l, r] = jnp.zeros((MODES, 128), F32)
        O2[l, r] = jnp.zeros((32, 128), F32)

    loop(6 * HIGH_ROWS, clear)
    own = U.at[:, pl.ds(0, OWN)]
    pltpu.make_async_copy(own, own, loc.at[3]).wait()

    def mix(matrix, a, b):
        u = jnp.concatenate([a, b], axis=1)
        u = jnp.concatenate([u, jnp.zeros((8, 256), F32)], axis=0)
        high = u.astype(BF16)
        low = (u - high.astype(F32)).astype(BF16)
        return jnp.dot(
            matrix[...], jnp.concatenate([high, low, high, low], axis=0), preferred_element_type=F32
        )

    def face_sum(row, d, v):
        total = None
        for k in range(TERMS):
            term = FC2[pl.ds(row * 36 + d * 6 + k, 1), :] * v[k]
            total = term if total is None else total + term
        return total

    lane8 = lax.broadcasted_iota(jnp.int32, (8, 128), 1)

    def apply_chunk(src, O, matrix, tiles, c):
        def pair(p):
            i = p // 2
            l = 2 * lax.rem(p, 2)
            r = chunk_row(c) + i
            base = c * (MODES * LAYERS * NR) + l * NR + i
            full = mix(
                matrix,
                src[pl.ds(base, MODES, stride=LAYERS * NR), :],
                src[pl.ds(base + NR, MODES, stride=LAYERS * NR), :],
            )
            for h in range(2):
                at_l, at_r, row = l + 1 + h, r + 1, (l + h) * ROWS + r
                for t in range(tiles):
                    v = [full[t * 48 + k * 8 : t * 48 + k * 8 + 8, h * 128 : h * 128 + 128] for k in range(TERMS)]
                    xl, xr, yl, yr, zl, zr = [face_sum(row, d, v) for d in range(FACES)]
                    zl_moved = jnp.where(lane8 == 127, 0.0, pltpu.roll(zl, 127, 1))
                    zr_moved = jnp.where(lane8 == 0, 0.0, pltpu.roll(zr, 1, 1))
                    tile = pl.ds(t * 8, 8)
                    O[at_l, at_r, tile, :] += (xl + xr) + (yl + yr) + ((zl + zr) - (zl_moved + zr_moved))
                    O[at_l - 1, at_r, tile, :] -= xl
                    O[at_l + 1, at_r, tile, :] -= xr
                    O[at_l, at_r - 1, tile, :] -= yl
                    O[at_l, at_r + 1, tile, :] -= yr

        loop(2 * NR, pair)

    def borders(n):
        O, XB, YB, count = ((O1, XB1, YB1, MODES), (O2, XB2, YB2, SIDE))[n]
        some = pl.ds(0, count)

        def x(up, c):
            l, slot, s = (LAYERS + 1, 0, 1) if up else (0, 1, -1)
            return send(
                O.at[l, pl.ds(chunk_row(c) + 1, NR), some],
                XB.at[slot, c, :, some],
                x_send.at[n, int(up)],
                x_recv.at[n, int(up), c],
                (near_peer, s_peer)[n](s),
            )

        def yy(up):
            r, slot, s = (ROWS + 1, 0, 1) if up else (0, 1, 3)
            return send(
                O.at[pl.ds(1, LAYERS), r, some],
                YB.at[slot, :, some],
                b_send.at[n, int(up)],
                b_recv.at[n, int(up)],
                y_peer(s),
            )

        return x, yy

    def is_top(c):
        return c == 1

    def is_bottom(c):
        return c == 0

    def send_borders(n, c):
        x, yy = borders(n)
        pl.when(has_high)(x(True, c).start)
        pl.when(has_low)(x(False, c).start)
        pl.when(jnp.logical_and(y_high, is_top(c)))(yy(True).start)
        pl.when(jnp.logical_and(y_low, is_bottom(c)))(yy(False).start)

    def add_borders(n, c):
        x, yy = borders(n)
        O, XB, YB, modes = ((O1, XB1, YB1, MODES), (O2, XB2, YB2, 32))[n]
        r = chunk_row(c) + 1

        @pl.when(has_low)
        def _():
            x(True, c).wait_recv()
            for i in range(NR):
                O[1, r + i] += XB[0, c, i]

        @pl.when(has_high)
        def _():
            x(False, c).wait_recv()
            for i in range(NR):
                O[LAYERS, r + i] += XB[1, c, i]

        @pl.when(jnp.logical_and(y_low, is_bottom(c)))
        def _():
            yy(True).wait_recv()
            for l in range(LAYERS):
                O[l + 1, 1] += YB[0, l]

        @pl.when(jnp.logical_and(y_high, is_top(c)))
        def _():
            yy(False).wait_recv()
            for l in range(LAYERS):
                O[l + 1, ROWS] += YB[1, l]

    def out_copy(n, step, c):
        to = lax.rem(y + step, 4)
        if n == 0:
            src, dst = F.at[c, pl.ds(zhi * SIDE + to * OWN, OWN)], first_out
        else:
            src, dst = S.at[c, pl.ds(to * OWN, OWN)], second_out
        dst = dst.at[:, :, pl.ds(y * ROWS + chunk_row(c), NR)]
        if step == 0:
            return pltpu.make_async_copy(src, dst, o_loc.at[n])
        return send(src, dst, o_send.at[n], o_recv.at[n], y_peer(step))

    def finish(n, c):
        add_borders(n, c)
        O, to, modes = ((O1, F2, MODES), (O2, S2, 32))[n]
        r = chunk_row(c) + 1
        for i in range(NR):
            for l in range(LAYERS):
                to[pl.ds(c * (modes * LAYERS * NR) + l * NR + i, modes, stride=LAYERS * NR), :] = O[l + 1, r + i]
        for step in (2, 1, 3, 0):
            out_copy(n, step, c).start()

    def stage(c):
        @pl.when(c < NC)
        def _():
            wait_z(c)
            apply_chunk(U2, O1, L1, 7, c)
            send_borders(0, c)

        @pl.when(c + AHEAD < NC)
        def _():
            y_to_z(c + AHEAD)

        @pl.when(jnp.logical_and(c >= LAG, c < NC + LAG))
        def _():
            finish(0, c - LAG)
            apply_chunk(F2, O2, L2, 4, c - LAG)
            send_borders(1, c - LAG)

        @pl.when(c >= 2 * LAG)
        def _():
            finish(1, c - 2 * LAG)

    loop(NC + 2 * LAG, stage)

    three = U.at[:, pl.ds(0, 3 * OWN)]
    side = U.at[:, pl.ds(0, SIDE)]
    send(three, three, y_send.at[0], y_recv.at[0], partner).wait_send()
    send(side, side, z_send.at[0], z_recv.at[0], partner).wait_send()
    for n in range(2):
        XB = (XB1, XB2)[n].at[0, :, :, pl.ds(0, (MODES, SIDE)[n])]
        for up, present in ((1, has_high), (0, has_low)):
            pl.when(present)(send(XB, XB, x_send.at[n, up], x_recv.at[n, up, 0], partner).wait_send)
    for n in range(2):
        _, yy = borders(n)
        pl.when(y_high)(yy(True).wait_send)
        pl.when(y_low)(yy(False).wait_send)
    pl.when(has_high)(a_copy(True).wait_send)
    pl.when(has_low)(a_copy(False).wait_send)
    for n in range(2):
        pltpu.make_async_copy(own, own, o_loc.at[n]).wait()
        every = send(three, three, o_send.at[n], o_recv.at[n], partner)
        every.wait_send()
        every.wait_recv()


def per_device(field, coeff, pairs, values):
    vmem = pl.BlockSpec(memory_space=pltpu.VMEM)
    hbm = pl.BlockSpec(memory_space=pl.ANY)
    out = jax.ShapeDtypeStruct((2, OWN, LAYERS, 48, 1, 128), F32)
    sem = pltpu.SemaphoreType.DMA
    both = pl.pallas_call(
        kernel,
        out_shape=out,
        in_specs=[hbm, hbm, vmem, vmem],
        out_specs=hbm,
        scratch_shapes=[
            pltpu.VMEM((NC, MODES, LAYERS, NR, 1, 128), F32),
            pltpu.VMEM((NC, MODES, LAYERS, NR, 1, 128), F32),
            pltpu.VMEM((NC, 32, LAYERS, NR, 1, 128), F32),
            pltpu.VMEM((2, NC, NR, MODES, 128), F32),
            pltpu.VMEM((2, NC, NR, 32, 128), F32),
            pltpu.VMEM((2, LAYERS, MODES, 128), F32),
            pltpu.VMEM((2, LAYERS, 32, 128), F32),
            pltpu.VMEM((TERMS + 1, 6, HIGH_ROWS, 1, 128), F32),
            pltpu.VMEM(((CELLS + 8) * 36, 1, 128), F32),
            pltpu.VMEM((6, HIGH_ROWS, MODES, 128), F32),
            pltpu.VMEM((6, HIGH_ROWS, 32, 128), F32),
            pltpu.VMEM((336, 256), F32),
            pltpu.VMEM((336, 256), BF16),
            pltpu.VMEM((192, 256), BF16),
            sem((1,)),
            sem((NC,)),
            sem((1,)),
            sem((NC,)),
            sem((2,)),
            sem((2,)),
            sem((2, 2)),
            sem((2, 2, NC)),
            sem((2, 2)),
            sem((2, 2)),
            sem((2,)),
            sem((2,)),
            sem((4,)),
            sem((2,)),
        ],
        compiler_params=pltpu.CompilerParams(
            collective_id=0, has_side_effects=True, vmem_limit_bytes=60 << 20
        ),
    )(
        field.reshape(OWN, LAYERS, 48, 1, 128),
        coeff.reshape(TERMS, LAYERS, 48, 1, 128),
        jnp.transpose(pairs, (0, 2, 1)),
        values,
    )
    def place(x, a, b):
        a[...] = x[0]
        b[...] = x[1]

    rows = OWN * LAYERS * 48
    flat = jax.ShapeDtypeStruct((rows, 128), F32)
    block = pl.BlockSpec((rows // 2, 128), lambda i: (i, 0))
    first, second = pl.pallas_call(
        place,
        grid=(2,),
        out_shape=(flat, flat),
        in_specs=[pl.BlockSpec((2, rows // 2, 128), lambda i: (0, i, 0))],
        out_specs=(block, block),
    )(both.reshape(2, rows, 128))
    return first.reshape(field.shape), second.reshape(field.shape)


def solution(mesh):
    in_specs = (P("mode", "space", None, None), P(None, "space", None, None), P(), P())
    out_specs = (P("mode", "space", None, None), P("mode", "space", None, None))
    return jax.shard_map(
        per_device, mesh=mesh, in_specs=in_specs, out_specs=out_specs, check_vma=False
    )
```

```python
import functools

import jax
import jax.numpy as jnp
from jax import lax
from jax.experimental import pallas as pl
from jax.experimental.pallas import tpu as pltpu
from jax.sharding import PartitionSpec as P

MESH = pl.DeviceIdType.MESH
F32 = jnp.float32
BF16 = jnp.bfloat16

TERMS = 6
OWN = 7
SIDE = 28
MODES = 56
LAYERS = 4
ROWS = 12
CELLS = LAYERS * ROWS
FACES = 6
HIGH_ROWS = ROWS + 2
NR = 1
NC = ROWS // NR
AHEAD = 5
AT_ONCE = 8
LAG = 4


def kernel(
    field,
    coeff,
    pairs,
    values,
    outs,
    U,
    F,
    S,
    XB1,
    XB2,
    YB1,
    YB2,
    A,
    FC,
    O1,
    O2,
    LF,
    L1,
    L2,
    y_send,
    y_recv,
    z_send,
    z_recv,
    c_send,
    c_recv,
    x_send,
    x_recv,
    b_send,
    b_recv,
    o_send,
    o_recv,
    loc,
    o_loc,
):
    first_out, second_out = outs.at[0], outs.at[1]
    space = lax.axis_index("space")
    mode = lax.axis_index("mode")
    y = mode // 2
    zhi = mode % 2

    def y_peer(step):
        return (space, lax.rem(y + step, 4) * 2 + zhi)

    partner = (space, y * 2 + 1 - zhi)

    def s_peer(step):
        return (space + step, mode)

    at_end = {1: space % 8 == 7, -1: space % 8 == 0}

    def near_peer(step):
        return (space + step, jnp.where(at_end[step], y * 2 + 1 - zhi, mode))

    def send(src, dst, ss, rs, dev):
        return pltpu.make_async_remote_copy(
            src_ref=src, dst_ref=dst, send_sem=ss, recv_sem=rs, device_id=dev, device_id_type=MESH
        )

    def loop(n, body):
        def step(i, carry):
            body(i)
            return carry

        lax.fori_loop(0, n, step, 0)

    has_low = space > 0
    has_high = space < 31
    y_low = y > 0
    y_high = y < 3

    def chunk_row(c):
        return NR * jnp.where(c % 2 == 0, c // 2, NC - 1 - c // 2)

    U2 = U.reshape(NC * MODES * LAYERS * NR, 128)
    F2 = F.reshape(NC * MODES * LAYERS * NR, 128)
    S2 = S.reshape(NC * 32 * LAYERS * NR, 128)
    A2 = A.reshape((TERMS + 1) * 6 * HIGH_ROWS, 128)
    FC2 = FC.reshape((CELLS + 8) * 36, 128)

    A2[...] = jnp.zeros(A2.shape, F32)

    barrier = pltpu.get_barrier_semaphore()
    for step in (1, 2, 3):
        pl.semaphore_signal(barrier, inc=1, device_id=y_peer(step), device_id_type=MESH)
    pl.semaphore_signal(barrier, inc=1, device_id=partner, device_id_type=MESH)

    expected = jnp.int32(4)
    for present, step in ((has_low, -1), (has_high, 1)):
        turned = jnp.logical_and(present, at_end[step])

        @pl.when(present)
        def _(step=step):
            pl.semaphore_signal(barrier, inc=1, device_id=s_peer(step), device_id_type=MESH)

        @pl.when(turned)
        def _(step=step):
            pl.semaphore_signal(barrier, inc=1, device_id=near_peer(step), device_id_type=MESH)

        expected = expected + present.astype(jnp.int32) + turned.astype(jnp.int32)
    pl.semaphore_wait(barrier, expected)

    def y_copy(step, c):
        to = lax.rem(y + step, 4)
        return send(
            field.at[:, :, pl.ds(to * ROWS + chunk_row(c), NR)],
            U.at[c, pl.ds(zhi * SIDE + y * OWN, OWN)],
            y_send.at[0],
            y_recv.at[c],
            y_peer(step),
        )

    def wait_y(c):
        three = U.at[c, pl.ds(0, 3 * OWN)]
        send(three, three, y_send.at[0], y_recv.at[c], partner).wait_recv()

    def own_rows(c):
        return field.at[:, :, pl.ds(y * ROWS + chunk_row(c), NR)]

    def z_copy(c, j):
        at = pl.ds(zhi * SIDE + lax.rem(y + j, 4) * OWN, OWN)
        src = own_rows(c) if j == 0 else U.at[c, at]
        return send(src, U.at[c, at], z_send.at[0], z_recv.at[c], partner)

    def wait_z(c):
        side = U.at[c, pl.ds((1 - zhi) * SIDE, SIDE)]
        send(side, side, z_send.at[0], z_recv.at[c], partner).wait_recv()

    def own_copy(c):
        return pltpu.make_async_copy(own_rows(c), U.at[c, pl.ds(zhi * SIDE + y * OWN, OWN)], loc.at[3])

    def start_field(c):
        for step in (2, 1, 3):
            y_copy(step, c).start()

        @pl.when(c < AT_ONCE)
        def _():
            z_copy(c, 0).start()

    loop(NC, start_field)

    own_a = pltpu.make_async_copy(
        coeff.at[:, :, pl.ds(y * ROWS, ROWS)], A.at[pl.ds(0, TERMS), pl.ds(1, LAYERS), pl.ds(1, ROWS)], loc.at[0]
    )
    low_a = pltpu.make_async_copy(
        coeff.at[:, :, pl.ds(jnp.maximum(y * ROWS - 1, 0), 1)],
        A.at[pl.ds(0, TERMS), pl.ds(1, LAYERS), pl.ds(0, 1)],
        loc.at[1],
    )
    high_a = pltpu.make_async_copy(
        coeff.at[:, :, pl.ds(jnp.minimum(y * ROWS + ROWS, 47), 1)],
        A.at[pl.ds(0, TERMS), pl.ds(1, LAYERS), pl.ds(ROWS + 1, 1)],
        loc.at[2],
    )

    def a_copy(up):
        l, slot, s = (LAYERS - 1, 0, 1) if up else (0, LAYERS + 1, -1)
        return send(
            coeff.at[:, l, pl.ds(y * ROWS, ROWS)],
            A.at[pl.ds(0, TERMS), slot, pl.ds(1, ROWS)],
            c_send.at[int(up)],
            c_recv.at[int(up)],
            near_peer(s),
        )

    own_a.start()
    pl.when(y_low)(low_a.start)
    pl.when(y_high)(high_a.start)
    pl.when(has_high)(a_copy(True).start)
    pl.when(has_low)(a_copy(False).start)

    loop(NC, lambda c: own_copy(c).start())

    def y_to_z(c):
        @pl.when(c >= AT_ONCE)
        def _():
            z_copy(c, 0).start()

        wait_y(c)
        for j in (1, 2, 3):
            z_copy(c, j).start()

    loop(AHEAD, y_to_z)

    def mode_id(at):
        side = (at >= SIDE).astype(jnp.int32)
        rest = at - SIDE * side
        block = sum((rest >= OWN * n).astype(jnp.int32) for n in (1, 2, 3))
        return rest + OWN * block + OWN * side

    nnz = values.shape[1]
    eye = lax.broadcasted_iota(jnp.int32, (nnz, nnz), 0) == lax.broadcasted_iota(jnp.int32, (nnz, nnz), 1)
    slot = lax.broadcasted_iota(jnp.int32, (nnz, 256), 1) % 64
    col_id = jnp.where(slot < MODES, mode_id(slot), -1)
    low_part = lax.broadcasted_iota(jnp.int32, (8, 256), 1) >= 128

    def build(tiles, start, count, target):
        at = lax.broadcasted_iota(jnp.int32, (tiles * 8, nnz), 0)
        ids = jnp.where(at < count, mode_id(at + start), -1)

        def term(k):
            both = pairs[k]
            cols = jnp.sum(jnp.where(eye, both[1:2, :], 0), axis=1, keepdims=True)
            left = jnp.where(ids == both[0:1, :], values[pl.ds(k, 1), :], 0.0)
            right = jnp.where(col_id == cols, 1.0, 0.0)
            full = jnp.dot(left, right, precision=lax.Precision.HIGHEST, preferred_element_type=F32)
            for t in range(tiles):
                part = full[t * 8 : t * 8 + 8]
                high = part.astype(BF16).astype(F32)
                LF[pl.ds(pl.multiple_of(t * 48 + k * 8, 8), 8), :] = jnp.where(low_part, part - high, high)

        loop(TERMS, term)
        target[...] = LF[0 : tiles * 48, :].astype(BF16)

    build(7, 0, MODES, L1)
    build(4, zhi * SIDE, SIDE, L2)

    own_a.wait()
    pl.when(y_low)(low_a.wait)
    pl.when(y_high)(high_a.wait)
    pl.when(has_low)(a_copy(True).wait_recv)
    pl.when(has_high)(a_copy(False).wait_recv)
    lanes = lax.broadcasted_iota(jnp.int32, (ROWS, 128), 1)

    def faces(i):
        k = i // LAYERS
        l = lax.rem(i, LAYERS)
        base = (k * 6 + l + 1) * HIGH_ROWS + 1
        a = A2[pl.ds(base, ROWS), :]
        near = (
            A2[pl.ds(base - HIGH_ROWS, ROWS), :],
            A2[pl.ds(base + HIGH_ROWS, ROWS), :],
            A2[pl.ds(base - 1, ROWS), :],
            A2[pl.ds(base + 1, ROWS), :],
            jnp.where(lanes == 0, 0.0, pltpu.roll(a, 1, 1)),
            jnp.where(lanes == 127, 0.0, pltpu.roll(a, 127, 1)),
        )
        for d in range(FACES):
            FC2[pl.ds(l * (ROWS * 36) + d * 6 + k, ROWS, stride=36), :] = 0.5 * (a + near[d])

    loop(TERMS * LAYERS, faces)

    def clear(i):
        l = i // HIGH_ROWS
        r = lax.rem(i, HIGH_ROWS)
        O1[l, r] = jnp.zeros((MODES, 128), F32)
        O2[l, r] = jnp.zeros((32, 128), F32)

    loop(6 * HIGH_ROWS, clear)
    own = U.at[:, pl.ds(0, OWN)]
    pltpu.make_async_copy(own, own, loc.at[3]).wait()

    def mix(matrix, a, b):
        u = jnp.concatenate([a, b], axis=1)
        u = jnp.concatenate([u, jnp.zeros((8, 256), F32)], axis=0)
        high = u.astype(BF16)
        low = (u - high.astype(F32)).astype(BF16)
        return jnp.dot(
            matrix[...], jnp.concatenate([high, low, high, low], axis=0), preferred_element_type=F32
        )

    def face_sum(row, d, v):
        total = None
        for k in range(TERMS):
            term = FC2[pl.ds(row * 36 + d * 6 + k, 1), :] * v[k]
            total = term if total is None else total + term
        return total

    lane8 = lax.broadcasted_iota(jnp.int32, (8, 128), 1)

    def apply_chunk(src, O, matrix, tiles, c):
        def pair(p):
            i = p // 2
            l = 2 * lax.rem(p, 2)
            r = chunk_row(c) + i
            base = c * (MODES * LAYERS * NR) + l * NR + i
            full = mix(
                matrix,
                src[pl.ds(base, MODES, stride=LAYERS * NR), :],
                src[pl.ds(base + NR, MODES, stride=LAYERS * NR), :],
            )
            for h in range(2):
                at_l, at_r, row = l + 1 + h, r + 1, (l + h) * ROWS + r
                for t in range(tiles):
                    v = [full[t * 48 + k * 8 : t * 48 + k * 8 + 8, h * 128 : h * 128 + 128] for k in range(TERMS)]
                    xl, xr, yl, yr, zl, zr = [face_sum(row, d, v) for d in range(FACES)]
                    zl_moved = jnp.where(lane8 == 127, 0.0, pltpu.roll(zl, 127, 1))
                    zr_moved = jnp.where(lane8 == 0, 0.0, pltpu.roll(zr, 1, 1))
                    tile = pl.ds(t * 8, 8)
                    O[at_l, at_r, tile, :] += (xl + xr) + (yl + yr) + ((zl + zr) - (zl_moved + zr_moved))
                    O[at_l - 1, at_r, tile, :] -= xl
                    O[at_l + 1, at_r, tile, :] -= xr
                    O[at_l, at_r - 1, tile, :] -= yl
                    O[at_l, at_r + 1, tile, :] -= yr

        loop(2 * NR, pair)

    def borders(n):
        O, XB, YB, count = ((O1, XB1, YB1, MODES), (O2, XB2, YB2, SIDE))[n]
        some = pl.ds(0, count)

        def x(up, c):
            l, slot, s = (LAYERS + 1, 0, 1) if up else (0, 1, -1)
            return send(
                O.at[l, pl.ds(chunk_row(c) + 1, NR), some],
                XB.at[slot, c, :, some],
                x_send.at[n, int(up)],
                x_recv.at[n, int(up), c],
                (near_peer, s_peer)[n](s),
            )

        def yy(up):
            r, slot, s = (ROWS + 1, 0, 1) if up else (0, 1, 3)
            return send(
                O.at[pl.ds(1, LAYERS), r, some],
                YB.at[slot, :, some],
                b_send.at[n, int(up)],
                b_recv.at[n, int(up)],
                y_peer(s),
            )

        return x, yy

    def is_top(c):
        return c == 1

    def is_bottom(c):
        return c == 0

    def send_borders(n, c):
        x, yy = borders(n)
        pl.when(has_high)(x(True, c).start)
        pl.when(has_low)(x(False, c).start)
        pl.when(jnp.logical_and(y_high, is_top(c)))(yy(True).start)
        pl.when(jnp.logical_and(y_low, is_bottom(c)))(yy(False).start)

    def add_borders(n, c):
        x, yy = borders(n)
        O, XB, YB, modes = ((O1, XB1, YB1, MODES), (O2, XB2, YB2, 32))[n]
        r = chunk_row(c) + 1

        @pl.when(has_low)
        def _():
            x(True, c).wait_recv()
            for i in range(NR):
                O[1, r + i] += XB[0, c, i]

        @pl.when(has_high)
        def _():
            x(False, c).wait_recv()
            for i in range(NR):
                O[LAYERS, r + i] += XB[1, c, i]

        @pl.when(jnp.logical_and(y_low, is_bottom(c)))
        def _():
            yy(True).wait_recv()
            for l in range(LAYERS):
                O[l + 1, 1] += YB[0, l]

        @pl.when(jnp.logical_and(y_high, is_top(c)))
        def _():
            yy(False).wait_recv()
            for l in range(LAYERS):
                O[l + 1, ROWS] += YB[1, l]

    def out_copy(n, step, c):
        to = lax.rem(y + step, 4)
        if n == 0:
            src, dst = F.at[c, pl.ds(zhi * SIDE + to * OWN, OWN)], first_out
        else:
            src, dst = S.at[c, pl.ds(to * OWN, OWN)], second_out
        dst = dst.at[:, :, pl.ds(y * ROWS + chunk_row(c), NR)]
        if step == 0:
            return pltpu.make_async_copy(src, dst, o_loc.at[n])
        return send(src, dst, o_send.at[n], o_recv.at[n], y_peer(step))

    def finish(n, c):
        add_borders(n, c)
        O, to, modes = ((O1, F2, MODES), (O2, S2, 32))[n]
        r = chunk_row(c) + 1
        for i in range(NR):
            for l in range(LAYERS):
                to[pl.ds(c * (modes * LAYERS * NR) + l * NR + i, modes, stride=LAYERS * NR), :] = O[l + 1, r + i]
        for step in (2, 1, 3, 0):
            out_copy(n, step, c).start()

    def stage(c):
        @pl.when(c < NC)
        def _():
            wait_z(c)
            apply_chunk(U2, O1, L1, 7, c)
            send_borders(0, c)

        @pl.when(c + AHEAD < NC)
        def _():
            y_to_z(c + AHEAD)

        @pl.when(jnp.logical_and(c >= LAG, c < NC + LAG))
        def _():
            finish(0, c - LAG)
            apply_chunk(F2, O2, L2, 4, c - LAG)
            send_borders(1, c - LAG)

        @pl.when(c >= 2 * LAG)
        def _():
            finish(1, c - 2 * LAG)

    loop(NC + 2 * LAG, stage)

    three = U.at[:, pl.ds(0, 3 * OWN)]
    side = U.at[:, pl.ds(0, SIDE)]
    send(three, three, y_send.at[0], y_recv.at[0], partner).wait_send()
    send(side, side, z_send.at[0], z_recv.at[0], partner).wait_send()
    for n in range(2):
        XB = (XB1, XB2)[n].at[0, :, :, pl.ds(0, (MODES, SIDE)[n])]
        for up, present in ((1, has_high), (0, has_low)):
            pl.when(present)(send(XB, XB, x_send.at[n, up], x_recv.at[n, up, 0], partner).wait_send)
    for n in range(2):
        _, yy = borders(n)
        pl.when(y_high)(yy(True).wait_send)
        pl.when(y_low)(yy(False).wait_send)
    pl.when(has_high)(a_copy(True).wait_send)
    pl.when(has_low)(a_copy(False).wait_send)
    for n in range(2):
        pltpu.make_async_copy(own, own, o_loc.at[n]).wait()
        every = send(three, three, o_send.at[n], o_recv.at[n], partner)
        every.wait_send()
        every.wait_recv()


def per_device(field, coeff, pairs, values):
    vmem = pl.BlockSpec(memory_space=pltpu.VMEM)
    hbm = pl.BlockSpec(memory_space=pl.ANY)
    out = jax.ShapeDtypeStruct((2, OWN, LAYERS, 48, 1, 128), F32)
    sem = pltpu.SemaphoreType.DMA
    both = pl.pallas_call(
        kernel,
        out_shape=out,
        in_specs=[hbm, hbm, vmem, vmem],
        out_specs=hbm,
        scratch_shapes=[
            pltpu.VMEM((NC, MODES, LAYERS, NR, 1, 128), F32),
            pltpu.VMEM((NC, MODES, LAYERS, NR, 1, 128), F32),
            pltpu.VMEM((NC, 32, LAYERS, NR, 1, 128), F32),
            pltpu.VMEM((2, NC, NR, MODES, 128), F32),
            pltpu.VMEM((2, NC, NR, 32, 128), F32),
            pltpu.VMEM((2, LAYERS, MODES, 128), F32),
            pltpu.VMEM((2, LAYERS, 32, 128), F32),
            pltpu.VMEM((TERMS + 1, 6, HIGH_ROWS, 1, 128), F32),
            pltpu.VMEM(((CELLS + 8) * 36, 1, 128), F32),
            pltpu.VMEM((6, HIGH_ROWS, MODES, 128), F32),
            pltpu.VMEM((6, HIGH_ROWS, 32, 128), F32),
            pltpu.VMEM((336, 256), F32),
            pltpu.VMEM((336, 256), BF16),
            pltpu.VMEM((192, 256), BF16),
            sem((1,)),
            sem((NC,)),
            sem((1,)),
            sem((NC,)),
            sem((2,)),
            sem((2,)),
            sem((2, 2)),
            sem((2, 2, NC)),
            sem((2, 2)),
            sem((2, 2)),
            sem((2,)),
            sem((2,)),
            sem((4,)),
            sem((2,)),
        ],
        compiler_params=pltpu.CompilerParams(
            collective_id=0, has_side_effects=True, vmem_limit_bytes=60 << 20
        ),
    )(
        field.reshape(OWN, LAYERS, 48, 1, 128),
        coeff.reshape(TERMS, LAYERS, 48, 1, 128),
        jnp.transpose(pairs, (0, 2, 1)),
        values,
    )
    def place(x, a, b):
        a[...] = x[0]
        b[...] = x[1]

    rows = OWN * LAYERS * 48
    flat = jax.ShapeDtypeStruct((rows, 128), F32)
    block = pl.BlockSpec((rows // 2, 128), lambda i: (i, 0))
    first, second = pl.pallas_call(
        place,
        grid=(2,),
        out_shape=(flat, flat),
        in_specs=[pl.BlockSpec((2, rows // 2, 128), lambda i: (0, i, 0))],
        out_specs=(block, block),
    )(both.reshape(2, rows, 128))
    return first.reshape(field.shape), second.reshape(field.shape)


def solution(mesh):
    in_specs = (P("mode", "space", None, None), P(None, "space", None, None), P(), P())
    out_specs = (P("mode", "space", None, None), P("mode", "space", None, None))
    return jax.shard_map(
        per_device, mesh=mesh, in_specs=in_specs, out_specs=out_specs, check_vma=False
    )
```
